512 devices in a mesh: prow: 32 (over z, y_lo), pcol: 16 (over y_hi, x, core).
Axes of the slice: x: 4, y: 4 (y_hi: 2, y_lo: 2; y = y_hi * 2 + y_lo), z: 16, core: 2. Of those that a mesh axis runs over, the one named last changes fastest.
Arguments:
- orb_valence: bfloat16 [16384, 1000], P(('prow', 'pcol')), may hold values from -1.75 to 1.75
- orb_conduction: bfloat16 [16384, 1000], P(('prow', 'pcol')), may hold values from -1.75 to 1.75
- screened: bfloat16 [16384, 16384], P('prow', 'pcol'), may hold values from -0.046875 to 0.046875
- bare: bfloat16 [16384, 16384], P('prow', 'pcol'), may hold values from -0.046875 to 0.046875
- panel_valence: int32 [128], replicated, may hold values from 0 to 999
- panel_conduction: int32 [128], replicated, may hold values from 0 to 999
Outputs:
- kernel_panel: float32 [12000, 128], P('prow', 'pcol')
The draws below stay inside these ranges and needn't reach their ends.
All inputs are finite; a program needn't handle non-finite values.
Results may differ from the reference program's by a relative error of at most 0.004.
Values may be sent and summed in bfloat16 or wider, within the bound.
A program may use at most 64 MiB of HBM per device.

```python
import jax
import jax.numpy as jnp

NMU = 16384
NV = 1000
NC = 1000
NCW = 12
NP = 128


def set_ends(entries, stream_key, smallest, largest):
    shape = entries.shape
    place = [jax.random.randint(jax.random.fold_in(stream_key, axis), (), 0, shape[axis]) for axis in range(len(shape))]
    entries = entries.at[tuple(place)].set(smallest)
    longest = shape.index(max(shape))
    place[longest] = (place[longest] + 1) % shape[longest]
    return entries.at[tuple(place)].set(largest)


def levels(rng, dims, shards, low, high):
    def one(dim, blocks):
        heights = jax.random.uniform(jax.random.fold_in(jax.random.fold_in(rng, 6), dim), (blocks,), jnp.float32, low / len(shards), high / len(shards))
        return jnp.repeat(jnp.exp(heights), dims[dim] // blocks).reshape((-1,) + (1,) * (len(dims) - dim - 1))

    level = one(*shards[0])
    for cut in shards[1:]:
        level = level * one(*cut)
    return level


def noise(key, shape, deviation, reach, cuts=(), kind=jnp.bfloat16):
    level = levels(key, shape, cuts, -0.22, 0.18) if cuts else 1.0
    values = jax.random.normal(key, shape, jnp.float32) * deviation * level
    return jnp.minimum(jnp.maximum(values, -reach), reach).astype(kind)


def setup_inputs(seed: int = 0) -> dict:
    arg_keys = jax.random.split(jax.random.key(seed), 7)
    orb_valence = noise(arg_keys[0], (NMU, NV), (NMU ** -0.125), 1.75, ((0, 512),))
    orb_conduction = noise(arg_keys[1], (NMU, NC), (NMU ** -0.125), 1.75, ((0, 512),))
    screened = noise(arg_keys[2], (NMU, NMU), NMU ** -0.5, 0.046875, ((0, 32), (1, 16)))
    bare = noise(arg_keys[3], (NMU, NMU), NMU ** -0.5, 0.046875, ((0, 32), (1, 16)))
    panel_valence = set_ends(jax.random.randint(arg_keys[4], (NP,), 0, NV), jax.random.fold_in(arg_keys[4], 1), 0, NV - 1).astype(jnp.int32)
    panel_conduction = set_ends(jax.random.randint(arg_keys[5], (NP,), 0, NC), jax.random.fold_in(arg_keys[5], 1), 0, NC - 1).astype(jnp.int32)
    return {"orb_valence": orb_valence, "orb_conduction": orb_conduction, "screened": screened, "bare": bare, "panel_valence": panel_valence, "panel_conduction": panel_conduction}


def reference(orb_valence, orb_conduction, screened, bare, panel_valence, panel_conduction):
    valence_pick = jnp.take(orb_valence, panel_valence, axis=1)
    conduction_pick = jnp.take(orb_conduction, panel_conduction, axis=1)
    conduction_low = orb_conduction[:, :NCW]
    pair_direct = (conduction_pick.astype(jnp.float32)[:, :, None] * conduction_low.astype(jnp.float32)[:, None, :]).astype(jnp.bfloat16).reshape(NMU, NP * NCW)
    pair_exchange = (valence_pick.astype(jnp.float32) * conduction_pick.astype(jnp.float32)).astype(jnp.bfloat16)
    direct_sum = jnp.dot(screened, pair_direct, preferred_element_type=jnp.float32)
    exchange_sum = jnp.dot(bare, pair_exchange, preferred_element_type=jnp.float32)
    combined = 2.0 * conduction_low.astype(jnp.float32)[:, None, :] * exchange_sum[:, :, None] - valence_pick.astype(jnp.float32)[:, :, None] * direct_sum.reshape(NMU, NP, NCW)
    combined = combined.astype(jnp.bfloat16)
    panel = jnp.einsum("mv,mjc->cvj", orb_valence.astype(jnp.float32), combined.astype(jnp.float32))
    return panel.reshape(NCW * NV, NP)
```

```python
import jax
import jax.numpy as jnp
from jax import lax
from jax.experimental import pallas as pl
from jax.experimental.pallas import tpu as pltpu
from jax.sharding import PartitionSpec as P

NCW = 12
NZ = 16
NCOL = 16
PTS = 32
ROWS = PTS * NCOL
COLS = 1024
NB = 1000
NBP = 1024
HALF = 6
SEG = 375
SEGP = 384
BF = jnp.bfloat16
F32 = jnp.float32
MESH = pl.DeviceIdType.MESH
NT = (((1,), (1,)), ((), ()))


def iota(shape, dim):
    return lax.broadcasted_iota(jnp.int32, shape, dim)


def onehot(mask):
    return jnp.where(mask, 1.0, 0.0).astype(BF)


def kernel(
    v_ref, c_ref, pv_ref, pc_ref, pvs_ref, w_ref, b_ref, out_ref,
    blk, cpad, g_all, got, picks, lows, low_f32, turned, left, left_e,
    w_all, b_all, send0, send1, recv0, recv1, panel, seg_out, seg_in, total, y_in,
    loc_sem, wb_ssem, wb_rsem, a_ssem, a_rsem, g_ssem, g_rsem, h_ssem, h_rsem,
    f_ssem, f_rsem, b_ssem, b_rsem, c_ssem, c_rsem, y_ssem, y_rsem,
):
    row = lax.axis_index("prow")
    col = lax.axis_index("pcol")
    z = lax.div(row, 2)
    ylo = lax.rem(row, 2)
    core = lax.rem(col, 2)
    chip = lax.div(col, 2)
    mate = col + 1 - 2 * core
    other_row = row + 1 - 2 * ylo

    def remote(src, dst, ssem, rsem, prow, pcol):
        return pltpu.make_async_remote_copy(
            src_ref=src, dst_ref=dst, send_sem=ssem, recv_sem=rsem,
            device_id={"prow": prow, "pcol": pcol}, device_id_type=MESH,
        )

    w_local = pltpu.make_async_copy(w_ref, w_all.at[core], loc_sem.at[0])
    b_local = pltpu.make_async_copy(b_ref, b_all.at[core], loc_sem.at[1])
    w_local.start()
    b_local.start()

    barrier = pltpu.get_barrier_semaphore()

    def greet(prow, pcol):
        pl.semaphore_signal(barrier, inc=1, device_id={"prow": prow, "pcol": pcol}, device_id_type=MESH)

    def greet_step(i, _):
        @pl.when((i != z) | (col != z))
        def _():
            greet(2 * i + ylo, z)

        @pl.when((i != col) | (col != z))
        def _():
            greet(2 * col + ylo, i)

        @pl.when(i != col)
        def _():
            greet(row, i)

        @pl.when(i != z)
        def _():
            greet(2 * i + ylo, col)

        return 0

    lax.fori_loop(0, NZ, greet_step, 0)
    greet(other_row, col)
    greet(other_row, mate)

    val = v_ref[...]
    con = c_ref[...]
    bands = iota((NB, 128), 0)
    lanes = iota((NB, 128), 1)
    vp = jnp.dot(val, onehot(bands == pv_ref[...]), preferred_element_type=F32)
    cp = jnp.dot(con, onehot(bands == pc_ref[...]), preferred_element_type=F32)
    lane = iota((PTS, 128), 1)
    blk[0:PTS, :] = jnp.where(lane < 64, cp, pltpu.roll(vp, 64, 1)).astype(BF)
    blk[PTS : 2 * PTS, :] = jnp.where(lane < 64, pltpu.roll(cp, 64, 1), vp).astype(BF)
    cpad[...] = jnp.zeros((128, NB), BF)
    cpad[pl.ds(pl.multiple_of(lax.rem(col, 4) * PTS, PTS), PTS), :] = con
    low_rows = iota((16, NB), 0)
    low_sel = onehot((low_rows == iota((16, NB), 1)) & (low_rows < NCW))
    blk[2 * PTS :, :] = lax.dot_general(low_sel, cpad[...], NT, preferred_element_type=F32).astype(BF)
    tail = jnp.dot(val, onehot((bands == lanes + 896) & (lanes < 104)), preferred_element_type=F32)
    tail = tail + jnp.dot(con, onehot((bands + 104 == lanes) & (bands < NCW)), preferred_element_type=F32)
    g_all[pl.ds(col, 1), :, 0:896] = val[:, 0:896].reshape(1, PTS, 896)
    g_all[pl.ds(col, 1), :, 896:NBP] = tail.astype(BF).reshape(1, PTS, 128)

    w_local.wait()
    b_local.wait()
    same = jnp.where(col == z, 2, 0)
    pl.semaphore_wait(barrier, 64 - same)

    def a_copy(i):
        return remote(blk, got.at[col], a_ssem.at[i], a_rsem.at[col], 2 * i + ylo, z)

    def a_start(i, _):
        there = lax.rem(z + 8 + i, NZ)

        @pl.when((there != z) | (col != z))
        def _():
            a_copy(there).start()

        return 0

    lax.fori_loop(0, NZ, a_start, 0)

    @pl.when(col == z)
    def _():
        got[pl.ds(col, 1)] = blk[...].reshape(1, 80, 128)

    w_copy = remote(w_ref, w_all.at[core], wb_ssem.at[0], wb_rsem.at[0], row, mate)
    b_copy = remote(b_ref, b_all.at[core], wb_ssem.at[1], wb_rsem.at[1], row, mate)
    w_copy.start()
    b_copy.start()

    def g_copy(k):
        return remote(g_all.at[col], g_all.at[col], g_ssem.at[k], g_rsem.at[chip], row, 2 * k + core)

    def g_start(i, _):
        there = lax.rem(chip + i, 8)
        g_copy(there).start()
        return 0

    lax.fori_loop(1, 8, g_start, 0)

    def h_copy(k, mine):
        slot = 2 * k + mine
        return remote(g_all.at[slot], g_all.at[slot], h_ssem.at[k], h_rsem.at[k], row, mate)

    h_copy(chip, core).start()

    def a_recv(i, _):
        @pl.when((i != col) | (col != z))
        def _():
            remote(blk, got.at[i], a_ssem.at[i], a_rsem.at[i], row, mate).wait_recv()

        return 0

    lax.fori_loop(0, NCOL, a_recv, 0)

    def pick_own(i, _):
        picks[core, ylo, pl.ds(i, 1)] = got[pl.ds(i, 1), pl.ds(pl.multiple_of(core * PTS, PTS), PTS), :]
        return 0

    lax.fori_loop(0, NCOL, pick_own, 0)
    for g in range(4):
        part = got[4 * g, 64:80, :].astype(F32)
        for s in range(1, 4):
            part = part + got[4 * g + s, 64:80, :].astype(F32)
        lows[core, ylo, :, g * 128 : (g + 1) * 128] = part.astype(BF)

    there_half = got.at[:, pl.ds(pl.multiple_of((1 - core) * PTS, PTS), PTS), :]
    own_half = picks.at[core, ylo]
    own_low = lows.at[core, ylo]
    slot = core * 2 + ylo
    passes = []
    for n, (src, prow, pcol) in enumerate(
        ((there_half, row, mate), (own_half, other_row, col), (there_half, other_row, mate))
    ):
        passes.append(remote(src, picks.at[core, ylo], f_ssem.at[0, n], f_rsem.at[0, slot], prow, pcol))
        passes.append(remote(own_low, lows.at[core, ylo], f_ssem.at[1, n], f_rsem.at[1, slot], prow, pcol))
    for copy in passes:
        copy.start()

    def h_start(i, _):
        k = lax.rem(chip + i, 8)
        remote(g_all.at[col], g_all.at[2 * k + core], g_ssem.at[k], g_rsem.at[k], row, mate).wait_recv()
        h_copy(k, core).start()
        return 0

    lax.fori_loop(1, 8, h_start, 0)

    for n in range(4):
        @pl.when(slot != n)
        def _(n=n):
            a, b = n // 2, n % 2
            remote(own_half, picks.at[a, b], f_ssem.at[0, 0], f_rsem.at[0, n], row, mate).wait_recv()
            remote(own_low, lows.at[a, b], f_ssem.at[1, 0], f_rsem.at[1, n], row, mate).wait_recv()

    eye = onehot(iota((128, 128), 0) == iota((128, 128), 1))
    for n in range(4):
        a, b = n // 2, n % 2
        turned[:, n * ROWS : (n + 1) * ROWS] = lax.dot_general(
            eye, picks[a, b].reshape(ROWS, 128), NT, preferred_element_type=F32
        )
        low_f32[:, n * ROWS : (n + 1) * ROWS] = lows[a, b].astype(F32)

    w_copy.wait_recv()
    b_copy.wait_recv()
    left_e[...] = (turned[0:64, :] * turned[64:128, :]).astype(BF)

    def against(lhs, rhs, n):
        rows = pl.ds(pl.multiple_of(n * 256, 256), 256)
        return lax.dot_general(lhs[:, 0:COLS], rhs[0, rows, :], NT, preferred_element_type=F32) + lax.dot_general(
            lhs[:, COLS:], rhs[1, rows, :], NT, preferred_element_type=F32
        )

    far = 1 - lax.div(z, 8)

    def build(half):
        def step(m, _):
            tile = turned[pl.ds(pl.multiple_of(m * 8, 8), 8), :]
            for p in range(HALF // 2):
                first = half * HALF + 2 * p
                pair = jnp.concatenate(
                    [tile * low_f32[pl.ds(first, 1), :], tile * low_f32[pl.ds(first + 1, 1), :]], axis=0
                )
                left[pl.ds(pl.multiple_of(m * 48 + 16 * p, 16), 16), :] = pair.astype(BF)
            return 0

        lax.fori_loop(0, 8, step, 0)

    def b_copy_to(n, m):
        sends, recvs = ((send0, recv0), (send1, recv1))[n]
        return remote(sends.at[m], recvs.at[chip], b_ssem.at[n, m], b_rsem.at[n, chip], row, 8 * core + m)

    order = (far, 1 - far)
    for n in range(2):
        sends, recvs = ((send0, recv0), (send1, recv1))[n]
        build(order[n])

        def mul(t, _, n=n, sends=sends):
            span = pl.ds(pl.multiple_of(t * 256, 256), 256)
            d = against(left[...], w_all, t).astype(BF)
            for m in range(8):
                sends[m, 0:48, span] = d[m * 48 : (m + 1) * 48, :]
            if n == 0:
                e = against(left_e[...], b_all, t)
                head = e.astype(BF).astype(F32)
                rest = e - head
                for m in range(8):
                    both = jnp.concatenate([head[m * 8 : m * 8 + 8], rest[m * 8 : m * 8 + 8]], axis=0)
                    sends[m, 48:64, span] = both.astype(BF)
            return 0

        lax.fori_loop(0, 2, mul, 0)

        def b_start(m, _, n=n, sends=sends, recvs=recvs):
            @pl.when(8 * core + m != col)
            def _():
                b_copy_to(n, m).start()

            @pl.when(8 * core + m == col)
            def _():
                recvs[pl.ds(chip, 1)] = sends[pl.ds(m, 1)]

            return 0

        lax.fori_loop(0, 8, b_start, 0)

    def h_wait(i, _):
        h_copy(i, 1 - core).wait_recv()
        return 0

    lax.fori_loop(0, 8, h_wait, 0)
    points = g_all[...].reshape(ROWS, NBP)
    mine = jnp.zeros((8, NBP), jnp.int32)
    for i in range(8):
        mine = jnp.where(iota((8, NBP), 0) == i, pvs_ref[col * 8 + i], mine)
    sel = onehot(mine == iota((8, NBP), 1))
    vpt = lax.dot_general(sel, points, NT, preferred_element_type=F32)
    sel = onehot((iota((16, NBP), 1) == iota((16, NBP), 0) + NB) & (iota((16, NBP), 0) < NCW))
    low_f32[:, 0:ROWS] = lax.dot_general(sel, points, NT, preferred_element_type=F32)

    def b_recv(n):
        recvs = (recv0, recv1)[n]

        def step(k, _):
            @pl.when(2 * k + lax.div(col, 8) != col)
            def _():
                remote(recvs.at[k], recvs.at[k], b_ssem.at[n, 0], b_rsem.at[n, k], row, mate).wait_recv()

            return 0

        lax.fori_loop(0, 8, step, 0)

    def c_copy(i):
        return remote(seg_out.at[i], seg_in.at[z], c_ssem.at[i], c_rsem.at[z], 2 * i + ylo, col)

    lane = iota((8, SEGP), 1)
    for n in range(2):
        recvs = (recv0, recv1)[n]
        half = order[n]
        b_recv(n)
        d = recvs[0].astype(F32)
        for k in range(1, 8):
            d = d + recvs[k].astype(F32)
        if n == 0:
            exch = 2.0 * (d[48:56] + d[56:64])
        comb = [
            low_f32[pl.ds(half * HALF + i, 1), 0:ROWS] * exch - vpt * d[i * 8 : i * 8 + 8] for i in range(HALF)
        ]
        comb = jnp.concatenate(comb, axis=0).astype(BF)
        panel[...] = jnp.dot(comb, points, preferred_element_type=F32)
        for zl in range(8):
            halves = []
            for y in range(2):
                start = SEG * (2 * zl + y)
                band0, off = start // NB, start % NB
                seg = panel[band0 * 8 : band0 * 8 + 8, :]
                if off:
                    seg = pltpu.roll(seg, NBP - off, 1)
                seg = seg[:, 0:SEGP]
                if off + SEG > NB:
                    more = pltpu.roll(panel[band0 * 8 + 8 : band0 * 8 + 16, :], NB - off, 1)[:, 0:SEGP]
                    seg = jnp.where(lane < NB - off, seg, more)
                halves.append(seg)
            seg_out[pl.ds(half * 8 + zl, 1)] = jnp.concatenate(halves, axis=0).astype(BF).reshape(1, 16, SEGP)

        def c_start(i, _, half=half):
            there = half * 8 + i

            @pl.when(there != z)
            def _():
                c_copy(there).start()

            @pl.when(there == z)
            def _():
                seg_in[pl.ds(z, 1)] = seg_out[pl.ds(z, 1)]

            return 0

        lax.fori_loop(0, 8, c_start, 0)

    def c_recv(i, _):
        @pl.when(i != z)
        def _():
            remote(seg_out.at[i], seg_in.at[i], c_ssem.at[i], c_rsem.at[i], row, mate).wait_recv()

        return 0

    lax.fori_loop(0, NZ, c_recv, 0)
    acc = seg_in[0].astype(F32)
    for i in range(1, NZ):
        acc = acc + seg_in[i].astype(F32)
    total[...] = acc.reshape(2, 8, SEGP)
    y_copy = remote(total.at[1 - ylo], y_in, y_ssem, y_rsem, other_row, col)
    y_copy.start()

    def drain(i, _):
        @pl.when((i != z) | (col != z))
        def _():
            a_copy(i).wait_send()

        @pl.when(i != z)
        def _():
            c_copy(i).wait_send()

        return 0

    lax.fori_loop(0, NZ, drain, 0)

    def drain8(i, _):
        @pl.when(i != chip)
        def _():
            g_copy(i).wait_send()

        h_copy(i, core).wait_send()

        @pl.when(8 * core + i != col)
        def _():
            b_copy_to(0, i).wait_send()
            b_copy_to(1, i).wait_send()

        return 0

    lax.fori_loop(0, 8, drain8, 0)
    for copy in passes:
        copy.wait_send()
    w_copy.wait_send()
    b_copy.wait_send()
    y_copy.wait()
    out_ref[...] = total[ylo] + y_in[...]


def body(orb_valence, orb_conduction, screened, bare, panel_valence, panel_conduction):
    vmem = pl.BlockSpec(memory_space=pltpu.VMEM)
    hbm = pl.BlockSpec(memory_space=pl.ANY)
    dma = pltpu.SemaphoreType.DMA
    out = pl.pallas_call(
        kernel,
        out_shape=jax.ShapeDtypeStruct((8, SEGP), F32),
        in_specs=[vmem, vmem, vmem, vmem, pl.BlockSpec(memory_space=pltpu.SMEM), hbm, hbm],
        out_specs=vmem,
        scratch_shapes=[
            pltpu.VMEM((80, 128), BF),
            pltpu.VMEM((128, NB), BF),
            pltpu.VMEM((NCOL, PTS, NBP), BF),
            pltpu.VMEM((NCOL, 80, 128), BF),
            pltpu.VMEM((2, 2, NCOL, PTS, 128), BF),
            pltpu.VMEM((2, 2, 16, ROWS), BF),
            pltpu.VMEM((16, 2 * COLS), F32),
            pltpu.VMEM((128, 2 * COLS), F32),
            pltpu.VMEM((8 * HALF * 8, 2 * COLS), BF),
            pltpu.VMEM((64, 2 * COLS), BF),
            pltpu.VMEM((2, ROWS, COLS), BF),
            pltpu.VMEM((2, ROWS, COLS), BF),
            pltpu.VMEM((8, 64, ROWS), BF),
            pltpu.VMEM((8, 48, ROWS), BF),
            pltpu.VMEM((8, 64, ROWS), BF),
            pltpu.VMEM((8, 48, ROWS), BF),
            pltpu.VMEM((48, NBP), F32),
            pltpu.VMEM((NZ, 16, SEGP), BF),
            pltpu.VMEM((NZ, 16, SEGP), BF),
            pltpu.VMEM((2, 8, SEGP), F32),
            pltpu.VMEM((8, SEGP), F32),
            dma((2,)),
            dma((2,)), dma((2,)),
            dma((16,)), dma((16,)),
            dma((8,)), dma((8,)),
            dma((8,)), dma((8,)),
            dma((2, 3)), dma((2, 4)),
            dma((2, 8)), dma((2, 8)),
            dma((16,)), dma((16,)),
            dma, dma,
        ],
        compiler_params=pltpu.CompilerParams(
            collective_id=0, has_side_effects=True, vmem_limit_bytes=48 * 2**20
        ),
        name="kernel_panel",
    )(
        orb_valence, orb_conduction, panel_valence.reshape(1, -1), panel_conduction.reshape(1, -1),
        panel_valence, screened, bare,
    )
    return out[:, :SEG].T


def solution(mesh):
    placed = (
        P(("prow", "pcol"), None),
        P(("prow", "pcol"), None),
        P("prow", "pcol"),
        P("prow", "pcol"),
        P(),
        P(),
    )
    return jax.shard_map(
        body, mesh=mesh, in_specs=placed, out_specs=P("prow", "pcol"), check_vma=False
    )
```

```python
import jax
import jax.numpy as jnp
from jax import lax
from jax.experimental import pallas as pl
from jax.experimental.pallas import tpu as pltpu
from jax.sharding import PartitionSpec as P

NCW = 12
NZ = 16
NCOL = 16
PTS = 32
ROWS = PTS * NCOL
COLS = 1024
NB = 1000
NBP = 1024
HALF = 6
SEG = 375
SEGP = 384
HUBS = (0, 3, -3, 6, -6)
SECOND = tuple((n, d) for n in range(5) for d in ((-1, 0, 1, 2) if n == 3 else (-1, 0, 1)))
BF = jnp.bfloat16
F32 = jnp.float32
MESH = pl.DeviceIdType.MESH
NT = (((1,), (1,)), ((), ()))


def iota(shape, dim):
    return lax.broadcasted_iota(jnp.int32, shape, dim)


def onehot(mask):
    return jnp.where(mask, 1.0, 0.0).astype(BF)


def kernel(
    v_hbm, c_hbm, pv_hbm, pc_hbm, w_ref, b_ref, out_ref,
    v_ref, c_ref, pv_ref, pc_ref,
    hub, cpad, g_all, got, picks, lows, low_f32, turned, left, left_e,
    w_all, b_all, send0, send1, recv0, recv1, panel, seg_out, seg_in, total, y_in,
    loc_sem, wb_ssem, wb_rsem, a_ssem, a_rsem, s_ssem, s_rsem, g_ssem, g_rsem, h_ssem, h_rsem,
    f_ssem, f_rsem, b_ssem, b_rsem, c_ssem, c_rsem, y_ssem, y_rsem,
):
    row = lax.axis_index("prow")
    col = lax.axis_index("pcol")
    z = lax.div(row, 2)
    ylo = lax.rem(row, 2)
    core = lax.rem(col, 2)
    chip = lax.div(col, 2)
    mate = col + 1 - 2 * core
    other_row = row + 1 - 2 * ylo

    def around(i):
        return lax.rem(i + NZ, NZ)

    def remote(src, dst, ssem, rsem, prow, pcol):
        return pltpu.make_async_remote_copy(
            src_ref=src, dst_ref=dst, send_sem=ssem, recv_sem=rsem,
            device_id={"prow": prow, "pcol": pcol}, device_id_type=MESH,
        )

    loads = [
        pltpu.make_async_copy(src, dst, loc_sem.at[n])
        for n, (src, dst) in enumerate(
            ((c_hbm, c_ref), (pc_hbm, pc_ref), (v_hbm, v_ref), (pv_hbm, pv_ref), (w_ref, w_all.at[0]), (b_ref, b_all.at[0]))
        )
    ]
    for copy in loads:
        copy.start()

    barrier = pltpu.get_barrier_semaphore()

    def greet(prow, pcol):
        pl.semaphore_signal(barrier, inc=1, device_id={"prow": prow, "pcol": pcol}, device_id_type=MESH)

    ahead = around(z - col)
    step = jnp.where(ahead == 8, 2, lax.rem(ahead + 1, 3) - 1)
    step = jnp.where(ahead > 8, 1 - lax.rem(17 - ahead, 3), step)
    hub_z = around(z - step)

    def self_step():
        return hub_z == z

    def greet_step(i, _):
        for y in range(2):
            @pl.when((2 * hub_z + y != row) | (i != col))
            def _(y=y):
                greet(2 * hub_z + y, i)

        @pl.when(i != col)
        def _():
            greet(row, i)

        @pl.when(i != z)
        def _():
            greet(2 * i + ylo, col)

        return 0

    lax.fori_loop(0, NZ, greet_step, 0)
    for n in range(1, 5):
        greet(2 * around(z - HUBS[n]) + ylo, col)
    greet(other_row, col)

    for copy in loads[:4]:
        copy.wait()
    val = v_ref[...]
    con = c_ref[...]
    bands = iota((NB, 128), 0)
    lanes = iota((NB, 128), 1)
    vp = jnp.dot(val, onehot(bands == pv_ref[...]), preferred_element_type=F32)
    cp = jnp.dot(con, onehot(bands == pc_ref[...]), preferred_element_type=F32)
    lane = iota((PTS, 128), 1)
    hub[0, 0:PTS, :] = jnp.where(lane < 64, cp, pltpu.roll(vp, 64, 1)).astype(BF)
    hub[0, PTS : 2 * PTS, :] = jnp.where(lane < 64, pltpu.roll(cp, 64, 1), vp).astype(BF)
    cpad[...] = jnp.zeros((128, NB), BF)
    cpad[pl.ds(pl.multiple_of(lax.rem(col, 4) * PTS, PTS), PTS), :] = con
    low_rows = iota((16, NB), 0)
    low_sel = onehot((low_rows == iota((16, NB), 1)) & (low_rows < NCW))
    hub[0, 2 * PTS :, :] = lax.dot_general(low_sel, cpad[...], NT, preferred_element_type=F32).astype(BF)
    pl.semaphore_wait(barrier, 67 - jnp.where(self_step(), 1, 0))

    def s_copy(n):
        return remote(hub.at[0], hub.at[n], s_ssem.at[n], s_rsem.at[n], 2 * around(z + HUBS[n]) + ylo, col)

    for n in (3, 4, 1, 2):
        s_copy(n).start()

    def a_copy(m, y):
        n, d = SECOND[m]
        plane = around(z - HUBS[n])
        return remote(
            hub.at[n], got.at[ylo, col], a_ssem.at[m, y], a_rsem.at[ylo, col], 2 * around(z + d) + y, plane
        )

    def a_to_self(m, y):
        n, d = SECOND[m]
        return (around(z - HUBS[n]) == col) & (ylo == y) if d == 0 else None

    def a_start(n):
        for m in range(len(SECOND)):
            if SECOND[m][0] == n:
                for y in range(2):
                    own = a_to_self(m, y)
                    if own is None:
                        a_copy(m, y).start()
                    else:
                        @pl.when(jnp.logical_not(own))
                        def _(m=m, y=y):
                            a_copy(m, y).start()

        @pl.when(around(z - HUBS[n]) == col)
        def _():
            got[pl.ds(ylo, 1), pl.ds(col, 1)] = hub[n].reshape(1, 1, 80, 128)

    a_start(0)

    tail = jnp.dot(val, onehot((bands == lanes + 896) & (lanes < 104)), preferred_element_type=F32)
    tail = tail + jnp.dot(con, onehot((bands + 104 == lanes) & (bands < NCW)), preferred_element_type=F32)
    g_all[pl.ds(col, 1), :, 0:896] = val[:, 0:896].reshape(1, PTS, 896)
    g_all[pl.ds(col, 1), :, 896:NBP] = tail.astype(BF).reshape(1, PTS, 128)

    def g_copy(k):
        return remote(g_all.at[col], g_all.at[col], g_ssem.at[k], g_rsem.at[chip], row, 2 * k + core)

    def g_start(i, _):
        there = lax.rem(chip + i, 8)
        g_copy(there).start()
        return 0

    lax.fori_loop(1, 8, g_start, 0)

    def h_copy(k, mine):
        slot = 2 * k + mine
        return remote(g_all.at[slot], g_all.at[slot], h_ssem.at[k], h_rsem.at[k], row, mate)

    h_copy(chip, core).start()

    w_copy = remote(w_ref, w_all.at[1], wb_ssem.at[0], wb_rsem.at[0], row, mate)
    b_copy = remote(b_ref, b_all.at[1], wb_ssem.at[1], wb_rsem.at[1], row, mate)
    w_copy.start()
    b_copy.start()

    for n in (1, 2, 3, 4):
        s_copy(n).wait_recv()
        a_start(n)

    passes = []
    for y in range(2):
        def a_recv(i, _, y=y):
            @pl.when((2 * hub_z + y != row) | (i != col))
            def _():
                remote(hub.at[0], got.at[y, i], a_ssem.at[0, 0], a_rsem.at[y, i], row, mate).wait_recv()

            return 0

        lax.fori_loop(0, NCOL, a_recv, 0)
        for g in range(4):
            part = got[y, 4 * g, 64:80, :].astype(F32)
            for s in range(1, 4):
                part = part + got[y, 4 * g + s, 64:80, :].astype(F32)
            lows[0, y, :, g * 128 : (g + 1) * 128] = part.astype(BF)
        half = got.at[y, :, pl.ds(pl.multiple_of((1 - core) * PTS, PTS), PTS), :]
        passes.append(remote(half, picks.at[y], f_ssem.at[0, y], f_rsem.at[0, y], row, mate))
        passes.append(remote(lows.at[0, y], lows.at[1, y], f_ssem.at[1, y], f_rsem.at[1, y], row, mate))
        passes[-2].start()
        passes[-1].start()

    def h_start(i, _):
        k = lax.rem(chip + i, 8)
        remote(g_all.at[col], g_all.at[2 * k + core], g_ssem.at[k], g_rsem.at[k], row, mate).wait_recv()
        h_copy(k, core).start()
        return 0

    lax.fori_loop(1, 8, h_start, 0)

    eye = onehot(iota((128, 128), 0) == iota((128, 128), 1))
    own_rows = pl.ds(pl.multiple_of(core * PTS, PTS), PTS)
    for n in range(4):
        a, y = n // 2, n % 2
        span = slice(n * ROWS, (n + 1) * ROWS)
        if a:
            passes[2 * y].wait_recv()
            passes[2 * y + 1].wait_recv()
        half = picks[y] if a else got[y, :, own_rows, :]
        turned[:, span] = lax.dot_general(eye, half.reshape(ROWS, 128), NT, preferred_element_type=F32)
        low_f32[:, span] = lows[a, y].astype(F32)

    loads[4].wait()
    loads[5].wait()
    w_copy.wait_recv()
    b_copy.wait_recv()
    left_e[...] = (turned[0:64, :] * turned[64:128, :]).astype(BF)

    def against(lhs, rhs, n):
        rows = pl.ds(pl.multiple_of(n * 256, 256), 256)
        return lax.dot_general(lhs[:, 0:COLS], rhs[0, rows, :], NT, preferred_element_type=F32) + lax.dot_general(
            lhs[:, COLS:], rhs[1, rows, :], NT, preferred_element_type=F32
        )

    far = 1 - lax.div(z, 8)

    def build(half):
        def step(m, _):
            tile = turned[pl.ds(pl.multiple_of(m * 8, 8), 8), :]
            for p in range(HALF // 2):
                first = half * HALF + 2 * p
                pair = jnp.concatenate(
                    [tile * low_f32[pl.ds(first, 1), :], tile * low_f32[pl.ds(first + 1, 1), :]], axis=0
                )
                left[pl.ds(pl.multiple_of(m * 48 + 16 * p, 16), 16), :] = pair.astype(BF)
            return 0

        lax.fori_loop(0, 8, step, 0)

    def b_copy_to(n, m):
        sends, recvs = ((send0, recv0), (send1, recv1))[n]
        return remote(sends.at[m], recvs.at[chip], b_ssem.at[n, m], b_rsem.at[n, chip], row, 8 * core + m)

    order = (far, 1 - far)
    for n in range(2):
        sends, recvs = ((send0, recv0), (send1, recv1))[n]
        build(order[n])

        def mul(t, _, n=n, sends=sends):
            span = pl.ds(pl.multiple_of(t * 256, 256), 256)
            d = against(left[...], w_all, t).astype(BF)
            for m in range(8):
                sends[m, 0:48, span] = d[m * 48 : (m + 1) * 48, :]
            if n == 0:
                e = against(left_e[...], b_all, t)
                head = e.astype(BF).astype(F32)
                rest = e - head
                for m in range(8):
                    both = jnp.concatenate([head[m * 8 : m * 8 + 8], rest[m * 8 : m * 8 + 8]], axis=0)
                    sends[m, 48:64, span] = both.astype(BF)
            return 0

        lax.fori_loop(0, 2, mul, 0)

        def b_start(m, _, n=n, sends=sends, recvs=recvs):
            @pl.when(8 * core + m != col)
            def _():
                b_copy_to(n, m).start()

            @pl.when(8 * core + m == col)
            def _():
                recvs[pl.ds(chip, 1)] = sends[pl.ds(m, 1)]

            return 0

        lax.fori_loop(0, 8, b_start, 0)

    def h_wait(i, _):
        h_copy(i, 1 - core).wait_recv()
        return 0

    lax.fori_loop(0, 8, h_wait, 0)
    points = g_all[...].reshape(ROWS, NBP)
    mine = jnp.where(iota((8, 128), 1) == col * 8 + iota((8, 128), 0), pv_ref[...].astype(F32), 0.0)
    sel = onehot(jnp.sum(mine, axis=1, keepdims=True) == iota((8, NBP), 1).astype(F32))
    vpt = lax.dot_general(sel, points, NT, preferred_element_type=F32)
    sel = onehot((iota((16, NBP), 1) == iota((16, NBP), 0) + NB) & (iota((16, NBP), 0) < NCW))
    low_f32[:, 0:ROWS] = lax.dot_general(sel, points, NT, preferred_element_type=F32)

    def b_recv(n):
        recvs = (recv0, recv1)[n]

        def step(k, _):
            @pl.when(2 * k + lax.div(col, 8) != col)
            def _():
                remote(recvs.at[k], recvs.at[k], b_ssem.at[n, 0], b_rsem.at[n, k], row, mate).wait_recv()

            return 0

        lax.fori_loop(0, 8, step, 0)

    def c_copy(i):
        return remote(seg_out.at[i], seg_in.at[z], c_ssem.at[i], c_rsem.at[z], 2 * i + ylo, col)

    lane = iota((8, SEGP), 1)
    for n in range(2):
        recvs = (recv0, recv1)[n]
        half = order[n]
        b_recv(n)
        d = recvs[0].astype(F32)
        for k in range(1, 8):
            d = d + recvs[k].astype(F32)
        if n == 0:
            exch = 2.0 * (d[48:56] + d[56:64])
        comb = [
            low_f32[pl.ds(half * HALF + i, 1), 0:ROWS] * exch - vpt * d[i * 8 : i * 8 + 8] for i in range(HALF)
        ]
        comb = jnp.concatenate(comb, axis=0).astype(BF)
        panel[...] = jnp.dot(comb, points, preferred_element_type=F32)
        for zl in range(8):
            halves = []
            for y in range(2):
                start = SEG * (2 * zl + y)
                band0, off = start // NB, start % NB
                seg = panel[band0 * 8 : band0 * 8 + 8, :]
                if off:
                    seg = pltpu.roll(seg, NBP - off, 1)
                seg = seg[:, 0:SEGP]
                if off + SEG > NB:
                    more = pltpu.roll(panel[band0 * 8 + 8 : band0 * 8 + 16, :], NB - off, 1)[:, 0:SEGP]
                    seg = jnp.where(lane < NB - off, seg, more)
                halves.append(seg)
            seg_out[pl.ds(half * 8 + zl, 1)] = jnp.concatenate(halves, axis=0).astype(BF).reshape(1, 16, SEGP)

        def c_start(i, _, half=half):
            there = half * 8 + i

            @pl.when(there != z)
            def _():
                c_copy(there).start()

            @pl.when(there == z)
            def _():
                seg_in[pl.ds(z, 1)] = seg_out[pl.ds(z, 1)]

            return 0

        lax.fori_loop(0, 8, c_start, 0)

    def c_recv(i, _):
        @pl.when(i != z)
        def _():
            remote(seg_out.at[i], seg_in.at[i], c_ssem.at[i], c_rsem.at[i], row, mate).wait_recv()

        return 0

    lax.fori_loop(0, NZ, c_recv, 0)
    acc = seg_in[0].astype(F32)
    for i in range(1, NZ):
        acc = acc + seg_in[i].astype(F32)
    total[...] = acc.reshape(2, 8, SEGP)
    y_copy = remote(total.at[1 - ylo], y_in, y_ssem, y_rsem, other_row, col)
    y_copy.start()

    def drain(i, _):
        @pl.when(i != z)
        def _():
            c_copy(i).wait_send()

        return 0

    lax.fori_loop(0, NZ, drain, 0)
    for n in range(1, 5):
        s_copy(n).wait_send()
    for m in range(len(SECOND)):
        for y in range(2):
            own = a_to_self(m, y)
            if own is None:
                a_copy(m, y).wait_send()
            else:
                @pl.when(jnp.logical_not(own))
                def _(m=m, y=y):
                    a_copy(m, y).wait_send()

    def drain8(i, _):
        @pl.when(i != chip)
        def _():
            g_copy(i).wait_send()

        h_copy(i, core).wait_send()

        @pl.when(8 * core + i != col)
        def _():
            b_copy_to(0, i).wait_send()
            b_copy_to(1, i).wait_send()

        return 0

    lax.fori_loop(0, 8, drain8, 0)
    for copy in passes:
        copy.wait_send()
    w_copy.wait_send()
    b_copy.wait_send()
    y_copy.wait()
    out_ref[...] = total[ylo] + y_in[...]


def body(orb_valence, orb_conduction, screened, bare, panel_valence, panel_conduction):
    vmem = pl.BlockSpec(memory_space=pltpu.VMEM)
    hbm = pl.BlockSpec(memory_space=pl.ANY)
    dma = pltpu.SemaphoreType.DMA
    out = pl.pallas_call(
        kernel,
        out_shape=jax.ShapeDtypeStruct((8, SEGP), F32),
        in_specs=[hbm] * 6,
        out_specs=vmem,
        scratch_shapes=[
            pltpu.VMEM((PTS, NB), BF),
            pltpu.VMEM((PTS, NB), BF),
            pltpu.VMEM((1, 128), jnp.int32),
            pltpu.VMEM((1, 128), jnp.int32),
            pltpu.VMEM((5, 80, 128), BF),
            pltpu.VMEM((128, NB), BF),
            pltpu.VMEM((NCOL, PTS, NBP), BF),
            pltpu.VMEM((2, NCOL, 80, 128), BF),
            pltpu.VMEM((2, NCOL, PTS, 128), BF),
            pltpu.VMEM((2, 2, 16, ROWS), BF),
            pltpu.VMEM((16, 2 * COLS), F32),
            pltpu.VMEM((128, 2 * COLS), F32),
            pltpu.VMEM((8 * HALF * 8, 2 * COLS), BF),
            pltpu.VMEM((64, 2 * COLS), BF),
            pltpu.VMEM((2, ROWS, COLS), BF),
            pltpu.VMEM((2, ROWS, COLS), BF),
            pltpu.VMEM((8, 64, ROWS), BF),
            pltpu.VMEM((8, 48, ROWS), BF),
            pltpu.VMEM((8, 64, ROWS), BF),
            pltpu.VMEM((8, 48, ROWS), BF),
            pltpu.VMEM((48, NBP), F32),
            pltpu.VMEM((NZ, 16, SEGP), BF),
            pltpu.VMEM((NZ, 16, SEGP), BF),
            pltpu.VMEM((2, 8, SEGP), F32),
            pltpu.VMEM((8, SEGP), F32),
            dma((6,)),
            dma((2,)), dma((2,)),
            dma((len(SECOND), 2)), dma((2, 16)),
            dma((5,)), dma((5,)),
            dma((8,)), dma((8,)),
            dma((8,)), dma((8,)),
            dma((2, 2)), dma((2, 2)),
            dma((2, 8)), dma((2, 8)),
            dma((16,)), dma((16,)),
            dma, dma,
        ],
        compiler_params=pltpu.CompilerParams(
            collective_id=0, has_side_effects=True, vmem_limit_bytes=60 * 2**20
        ),
        name="kernel_panel",
    )(
        orb_valence, orb_conduction, panel_valence.reshape(1, -1), panel_conduction.reshape(1, -1),
        screened, bare,
    )
    return out[:, :SEG].T


def solution(mesh):
    placed = (
        P(("prow", "pcol"), None),
        P(("prow", "pcol"), None),
        P("prow", "pcol"),
        P("prow", "pcol"),
        P(),
        P(),
    )
    return jax.shard_map(
        body, mesh=mesh, in_specs=placed, out_specs=P("prow", "pcol"), check_vma=False
    )
```

```python
import jax
import jax.numpy as jnp
from jax import lax
from jax.experimental import pallas as pl
from jax.experimental.pallas import tpu as pltpu
from jax.sharding import PartitionSpec as P

NCW = 12
NZ = 16
NCOL = 16
PTS = 32
ROWS = PTS * NCOL
COLS = 1024
NB = 1000
NBP = 1024
HALF = 6
SEG = 375
SEGP = 384
HUBS = (0, 3, -3, 6, -6)
SECOND = tuple((n, d) for n in range(5) for d in ((-1, 0, 1, 2) if n == 3 else (-1, 0, 1)))
BF = jnp.bfloat16
F32 = jnp.float32
MESH = pl.DeviceIdType.MESH
NT = (((1,), (1,)), ((), ()))


def iota(shape, dim):
    return lax.broadcasted_iota(jnp.int32, shape, dim)


def onehot(mask):
    return jnp.where(mask, 1.0, 0.0).astype(BF)


def kernel(
    v_hbm, c_hbm, pv_hbm, pc_hbm, w_ref, b_ref, out_ref,
    v_ref, c_ref, pv_ref, pc_ref,
    hub, cpad, g_all, swap_out, swap_in, got, low_f32, turned, left, left_e,
    w_all, b_all, send0, send1, recv0, recv1, panel, seg_out, seg_in, total, y_in,
    loc_sem, wb_ssem, wb_rsem, a_ssem, a_rsem, s_ssem, s_rsem, g_ssem, g_rsem, h_ssem, h_rsem,
    f_ssem, f_rsem, b_ssem, b_rsem, c_ssem, c_rsem, y_ssem, y_rsem,
):
    row = lax.axis_index("prow")
    col = lax.axis_index("pcol")
    z = lax.div(row, 2)
    ylo = lax.rem(row, 2)
    core = lax.rem(col, 2)
    chip = lax.div(col, 2)
    mate = col + 1 - 2 * core
    other_row = row + 1 - 2 * ylo

    def around(i):
        return lax.rem(i + NZ, NZ)

    def remote(src, dst, ssem, rsem, prow, pcol):
        return pltpu.make_async_remote_copy(
            src_ref=src, dst_ref=dst, send_sem=ssem, recv_sem=rsem,
            device_id={"prow": prow, "pcol": pcol}, device_id_type=MESH,
        )

    loads = [
        pltpu.make_async_copy(src, dst, loc_sem.at[n])
        for n, (src, dst) in enumerate(
            ((c_hbm, c_ref), (pc_hbm, pc_ref), (v_hbm, v_ref), (pv_hbm, pv_ref), (w_ref, w_all.at[core]), (b_ref, b_all.at[core]))
        )
    ]
    for copy in loads:
        copy.start()

    barrier = pltpu.get_barrier_semaphore()

    def greet(prow, pcol):
        pl.semaphore_signal(barrier, inc=1, device_id={"prow": prow, "pcol": pcol}, device_id_type=MESH)

    def step_of(plane):
        ahead = around(z - plane)
        back = 1 - lax.rem(17 - ahead, 3)
        return jnp.where(ahead > 8, back, jnp.where(ahead == 8, 2, lax.rem(ahead + 1, 3) - 1))

    hub_z = [around(z - step_of(2 * chip + e)) for e in range(2)]

    def greet_step(i, _):
        for e in range(2):
            for y in range(2):
                @pl.when((hub_z[e] != z) | (ylo != y) | (i != chip))
                def _(e=e, y=y):
                    greet(2 * hub_z[e] + y, 2 * i + core)

        return 0

    lax.fori_loop(0, 8, greet_step, 0)

    def greet_line(i, _):
        @pl.when(i != col)
        def _():
            greet(row, i)

        @pl.when(i != z)
        def _():
            greet(2 * i + ylo, col)

        return 0

    lax.fori_loop(0, NZ, greet_line, 0)
    for n in range(1, 5):
        greet(2 * around(z - HUBS[n]) + ylo, col)
    greet(other_row, col)

    for copy in loads[:4]:
        copy.wait()
    val = v_ref[...]
    con = c_ref[...]
    bands = iota((NB, 128), 0)
    lanes = iota((NB, 128), 1)
    vp = jnp.dot(val, onehot(bands == pv_ref[...]), preferred_element_type=F32)
    cp = jnp.dot(con, onehot(bands == pc_ref[...]), preferred_element_type=F32)
    lane = iota((PTS, 128), 1)
    first = jnp.where(lane < 64, cp, pltpu.roll(vp, 64, 1))
    second = jnp.where(lane < 64, pltpu.roll(cp, 64, 1), vp)
    cpad[...] = jnp.zeros((128, NB), BF)
    cpad[pl.ds(pl.multiple_of(lax.rem(col, 4) * PTS, PTS), PTS), :] = con
    low_rows = iota((16, NB), 0)
    low_sel = onehot((low_rows == iota((16, NB), 1)) & (low_rows < NCW))
    low = lax.dot_general(low_sel, cpad[...], NT, preferred_element_type=F32)
    swap_out[0:PTS, :] = jnp.where(core == 0, second, first).astype(BF)
    swap_out[PTS:, :] = low.astype(BF)
    own_pts = pl.ds(pl.multiple_of(core * PTS, PTS), PTS)
    mate_pts = pl.ds(pl.multiple_of((1 - core) * PTS, PTS), PTS)
    hub[0, own_pts, :] = jnp.where(core == 0, first, second).astype(BF)
    tail = jnp.dot(val, onehot((bands == lanes + 896) & (lanes < 104)), preferred_element_type=F32)
    tail = tail + jnp.dot(con, onehot((bands + 104 == lanes) & (bands < NCW)), preferred_element_type=F32)
    g_all[pl.ds(col, 1), :, 0:896] = val[:, 0:896].reshape(1, PTS, 896)
    g_all[pl.ds(col, 1), :, 896:NBP] = tail.astype(BF).reshape(1, PTS, 128)

    pl.semaphore_wait(barrier, 67 - jnp.where((hub_z[0] == z) | (hub_z[1] == z), 1, 0))
    def g_copy(k):
        return remote(g_all.at[col], g_all.at[col], g_ssem.at[k], g_rsem.at[chip], row, 2 * k + core)

    def g_start(i, _):
        there = lax.rem(chip + i, 8)
        g_copy(there).start()
        return 0

    lax.fori_loop(1, 8, g_start, 0)

    def h_copy(k, mine):
        slot = 2 * k + mine
        return remote(g_all.at[slot], g_all.at[slot], h_ssem.at[k], h_rsem.at[k], row, mate)

    h_copy(chip, core).start()

    swap = remote(swap_out, swap_in, f_ssem, f_rsem, row, mate)
    swap.start()
    swap.wait_recv()
    hub[0, mate_pts, :] = swap_in[0:PTS, :]
    hub[0, 2 * PTS :, :] = (low + swap_in[PTS:, :].astype(F32)).astype(BF)

    def s_copy(n):
        return remote(hub.at[0], hub.at[n], s_ssem.at[n], s_rsem.at[n], 2 * around(z + HUBS[n]) + ylo, col)

    for n in (3, 4, 1, 2):
        s_copy(n).start()

    def a_copy(m, y):
        n, d = SECOND[m]
        plane = around(z - HUBS[n])
        return remote(
            hub.at[n], got.at[lax.rem(plane, 2), ylo, chip], a_ssem.at[m, y], a_rsem.at[lax.rem(plane, 2), ylo, chip],
            2 * around(z + d) + y, 2 * lax.div(plane, 2) + core,
        )

    def own_plane(n):
        return lax.div(around(z - HUBS[n]), 2) == chip

    def a_to_self(m, y):
        n, d = SECOND[m]
        return own_plane(n) & (ylo == y) if d == 0 else None

    def a_start(n):
        for m in range(len(SECOND)):
            if SECOND[m][0] == n:
                for y in range(2):
                    own = a_to_self(m, y)
                    if own is None:
                        a_copy(m, y).start()
                    else:
                        @pl.when(jnp.logical_not(own))
                        def _(m=m, y=y):
                            a_copy(m, y).start()

        @pl.when(own_plane(n))
        def _():
            got[lax.rem(around(z - HUBS[n]), 2), ylo, chip] = hub[n]

    a_start(0)

    w_copy = remote(w_ref, w_all.at[core], wb_ssem.at[0], wb_rsem.at[0], row, mate)
    b_copy = remote(b_ref, b_all.at[core], wb_ssem.at[1], wb_rsem.at[1], row, mate)
    w_copy.start()
    b_copy.start()

    for n in (1, 2, 3, 4):
        s_copy(n).wait_recv()
        a_start(n)

    eye = onehot(iota((128, 128), 0) == iota((128, 128), 1))

    def arrive(e, y):
        def a_recv(i, _):
            @pl.when((hub_z[e] != z) | (ylo != y) | (i != chip))
            def _():
                remote(hub.at[0], got.at[e, y, i], a_ssem.at[0, 0], a_rsem.at[e, y, i], row, mate).wait_recv()

            return 0

        lax.fori_loop(0, 8, a_recv, 0)

    for e in range(2):
        for y in range(2):
            arrive(e, y)

    for e in range(2):
        for y in range(2):
            at = (2 * e + y) * ROWS
            rows = got[e, y, :, 0:64, :].reshape(ROWS, 128)
            turned[:, at : at + ROWS] = lax.dot_general(eye, rows, NT, preferred_element_type=F32)
            for g in range(4):
                low_f32[:, at + g * 128 : at + g * 128 + 128] = (
                    got[e, y, 2 * g, 64:80, :].astype(F32) + got[e, y, 2 * g + 1, 64:80, :].astype(F32)
                )

    loads[4].wait()
    loads[5].wait()
    w_copy.wait_recv()
    b_copy.wait_recv()
    left_e[...] = (turned[0:64, :] * turned[64:128, :]).astype(BF)

    def against(lhs, rhs, n):
        rows = pl.ds(pl.multiple_of(n * 256, 256), 256)
        return lax.dot_general(lhs[:, 0:COLS], rhs[0, rows, :], NT, preferred_element_type=F32) + lax.dot_general(
            lhs[:, COLS:], rhs[1, rows, :], NT, preferred_element_type=F32
        )

    def band_of(parity, i):
        return 3 * parity + i + 3 * (i // 3)

    def plane_of(parity, i):
        return 4 * parity + i + 4 * lax.div(i, 4)

    near = lax.rem(lax.div(z, 4), 2)

    def build(parity):
        def step(m, _):
            tile = turned[pl.ds(pl.multiple_of(m * 8, 8), 8), :]
            for p in range(HALF // 2):
                pair = jnp.concatenate(
                    [tile * low_f32[pl.ds(band_of(parity, 2 * p + k), 1), :] for k in range(2)], axis=0
                )
                left[pl.ds(pl.multiple_of(m * 48 + 16 * p, 16), 16), :] = pair.astype(BF)
            return 0

        lax.fori_loop(0, 8, step, 0)

    def b_copy_to(n, m):
        sends, recvs = ((send0, recv0), (send1, recv1))[n]
        return remote(sends.at[m], recvs.at[chip], b_ssem.at[n, m], b_rsem.at[n, chip], row, 8 * core + m)

    order = (near, 1 - near)
    for n in range(2):
        sends, recvs = ((send0, recv0), (send1, recv1))[n]
        build(order[n])

        def mul(t, _, n=n, sends=sends):
            span = pl.ds(pl.multiple_of(t * 256, 256), 256)
            d = against(left[...], w_all, t).astype(BF)
            for m in range(8):
                sends[m, 0:48, span] = d[m * 48 : (m + 1) * 48, :]
            if n == 0:
                e = against(left_e[...], b_all, t)
                head = e.astype(BF).astype(F32)
                rest = e - head
                for m in range(8):
                    both = jnp.concatenate([head[m * 8 : m * 8 + 8], rest[m * 8 : m * 8 + 8]], axis=0)
                    sends[m, 48:64, span] = both.astype(BF)
            return 0

        lax.fori_loop(0, 2, mul, 0)

        def b_start(m, _, n=n, sends=sends, recvs=recvs):
            @pl.when(8 * core + m != col)
            def _():
                b_copy_to(n, m).start()

            @pl.when(8 * core + m == col)
            def _():
                recvs[pl.ds(chip, 1)] = sends[pl.ds(m, 1)]

            return 0

        lax.fori_loop(0, 8, b_start, 0)

    def h_start(i, _):
        k = lax.rem(chip + i, 8)
        remote(g_all.at[col], g_all.at[2 * k + core], g_ssem.at[k], g_rsem.at[k], row, mate).wait_recv()
        h_copy(k, core).start()
        return 0

    lax.fori_loop(1, 8, h_start, 0)

    def h_wait(i, _):
        h_copy(i, 1 - core).wait_recv()
        return 0

    lax.fori_loop(0, 8, h_wait, 0)
    points = g_all[...].reshape(ROWS, NBP)
    mine = jnp.where(iota((8, 128), 1) == col * 8 + iota((8, 128), 0), pv_ref[...].astype(F32), 0.0)
    sel = onehot(jnp.sum(mine, axis=1, keepdims=True) == iota((8, NBP), 1).astype(F32))
    vpt = lax.dot_general(sel, points, NT, preferred_element_type=F32)
    sel = onehot((iota((16, NBP), 1) == iota((16, NBP), 0) + NB) & (iota((16, NBP), 0) < NCW))
    low_f32[:, 0:ROWS] = lax.dot_general(sel, points, NT, preferred_element_type=F32)

    def b_recv(n):
        recvs = (recv0, recv1)[n]

        def step(k, _):
            @pl.when(2 * k + lax.div(col, 8) != col)
            def _():
                remote(recvs.at[k], recvs.at[k], b_ssem.at[n, 0], b_rsem.at[n, k], row, mate).wait_recv()

            return 0

        lax.fori_loop(0, 8, step, 0)

    def c_copy(i):
        return remote(seg_out.at[i], seg_in.at[z], c_ssem.at[i], c_rsem.at[z], 2 * i + ylo, col)

    lane = iota((8, SEGP), 1)
    for n in range(2):
        recvs = (recv0, recv1)[n]
        parity = order[n]
        b_recv(n)
        d = recvs[0].astype(F32)
        for k in range(1, 8):
            d = d + recvs[k].astype(F32)
        if n == 0:
            exch = 2.0 * (d[48:56] + d[56:64])
        comb = [
            low_f32[pl.ds(band_of(parity, i), 1), 0:ROWS] * exch - vpt * d[i * 8 : i * 8 + 8] for i in range(HALF)
        ]
        comb = jnp.concatenate(comb, axis=0).astype(BF)
        panel[...] = jnp.dot(comb, points, preferred_element_type=F32)
        for zl in range(8):
            halves = []
            for y in range(2):
                start = SEG * (2 * zl + y)
                band0, off = start // NB, start % NB
                seg = panel[band0 * 8 : band0 * 8 + 8, :]
                if off:
                    seg = pltpu.roll(seg, NBP - off, 1)
                seg = seg[:, 0:SEGP]
                if off + SEG > NB:
                    more = pltpu.roll(panel[band0 * 8 + 8 : band0 * 8 + 16, :], NB - off, 1)[:, 0:SEGP]
                    seg = jnp.where(lane < NB - off, seg, more)
                halves.append(seg)
            seg_out[pl.ds(plane_of(parity, zl), 1)] = jnp.concatenate(halves, axis=0).astype(BF).reshape(1, 16, SEGP)

        def c_start(i, _, parity=parity):
            there = plane_of(parity, i)

            @pl.when(there != z)
            def _():
                c_copy(there).start()

            @pl.when(there == z)
            def _():
                seg_in[pl.ds(z, 1)] = seg_out[pl.ds(z, 1)]

            return 0

        lax.fori_loop(0, 8, c_start, 0)

    def c_recv(i, _):
        @pl.when(i != z)
        def _():
            remote(seg_out.at[i], seg_in.at[i], c_ssem.at[i], c_rsem.at[i], row, mate).wait_recv()

        return 0

    lax.fori_loop(0, NZ, c_recv, 0)
    acc = seg_in[0].astype(F32)
    for i in range(1, NZ):
        acc = acc + seg_in[i].astype(F32)
    total[...] = acc.reshape(2, 8, SEGP)
    y_copy = remote(total.at[1 - ylo], y_in, y_ssem, y_rsem, other_row, col)
    y_copy.start()

    def drain(i, _):
        @pl.when(i != z)
        def _():
            c_copy(i).wait_send()

        return 0

    lax.fori_loop(0, NZ, drain, 0)
    for n in range(1, 5):
        s_copy(n).wait_send()
    for m in range(len(SECOND)):
        for y in range(2):
            own = a_to_self(m, y)
            if own is None:
                a_copy(m, y).wait_send()
            else:
                @pl.when(jnp.logical_not(own))
                def _(m=m, y=y):
                    a_copy(m, y).wait_send()

    def drain8(i, _):
        @pl.when(i != chip)
        def _():
            g_copy(i).wait_send()

        h_copy(i, core).wait_send()

        @pl.when(8 * core + i != col)
        def _():
            b_copy_to(0, i).wait_send()
            b_copy_to(1, i).wait_send()

        return 0

    lax.fori_loop(0, 8, drain8, 0)
    swap.wait_send()
    w_copy.wait_send()
    b_copy.wait_send()
    y_copy.wait()
    out_ref[...] = total[ylo] + y_in[...]


def body(orb_valence, orb_conduction, screened, bare, panel_valence, panel_conduction):
    vmem = pl.BlockSpec(memory_space=pltpu.VMEM)
    hbm = pl.BlockSpec(memory_space=pl.ANY)
    dma = pltpu.SemaphoreType.DMA
    out = pl.pallas_call(
        kernel,
        out_shape=jax.ShapeDtypeStruct((8, SEGP), F32),
        in_specs=[hbm] * 6,
        out_specs=vmem,
        scratch_shapes=[
            pltpu.VMEM((PTS, NB), BF),
            pltpu.VMEM((PTS, NB), BF),
            pltpu.VMEM((1, 128), jnp.int32),
            pltpu.VMEM((1, 128), jnp.int32),
            pltpu.VMEM((5, 80, 128), BF),
            pltpu.VMEM((128, NB), BF),
            pltpu.VMEM((NCOL, PTS, NBP), BF),
            pltpu.VMEM((48, 128), BF),
            pltpu.VMEM((48, 128), BF),
            pltpu.VMEM((2, 2, 8, 80, 128), BF),
            pltpu.VMEM((16, 2 * COLS), F32),
            pltpu.VMEM((128, 2 * COLS), F32),
            pltpu.VMEM((8 * HALF * 8, 2 * COLS), BF),
            pltpu.VMEM((64, 2 * COLS), BF),
            pltpu.VMEM((2, ROWS, COLS), BF),
            pltpu.VMEM((2, ROWS, COLS), BF),
            pltpu.VMEM((8, 64, ROWS), BF),
            pltpu.VMEM((8, 48, ROWS), BF),
            pltpu.VMEM((8, 64, ROWS), BF),
            pltpu.VMEM((8, 48, ROWS), BF),
            pltpu.VMEM((48, NBP), F32),
            pltpu.VMEM((NZ, 16, SEGP), BF),
            pltpu.VMEM((NZ, 16, SEGP), BF),
            pltpu.VMEM((2, 8, SEGP), F32),
            pltpu.VMEM((8, SEGP), F32),
            dma((6,)),
            dma((2,)), dma((2,)),
            dma((len(SECOND), 2)), dma((2, 2, 8)),
            dma((5,)), dma((5,)),
            dma((8,)), dma((8,)),
            dma((8,)), dma((8,)),
            dma, dma,
            dma((2, 8)), dma((2, 8)),
            dma((16,)), dma((16,)),
            dma, dma,
        ],
        compiler_params=pltpu.CompilerParams(
            collective_id=0, has_side_effects=True, vmem_limit_bytes=60 * 2**20
        ),
        name="kernel_panel",
    )(
        orb_valence, orb_conduction, panel_valence.reshape(1, -1), panel_conduction.reshape(1, -1),
        screened, bare,
    )
    return out[:, :SEG].T


def solution(mesh):
    placed = (
        P(("prow", "pcol"), None),
        P(("prow", "pcol"), None),
        P("prow", "pcol"),
        P("prow", "pcol"),
        P(),
        P(),
    )
    return jax.shard_map(
        body, mesh=mesh, in_specs=placed, out_specs=P("prow", "pcol"), check_vma=False
    )
```

```python
import jax
import jax.numpy as jnp
from jax import lax
from jax.experimental import pallas as pl
from jax.experimental.pallas import tpu as pltpu
from jax.sharding import PartitionSpec as P

NCW = 12
NZ = 16
NCOL = 16
PTS = 32
ROWS = PTS * NCOL
COLS = 1024
NB = 1000
NBP = 1024
HALF = 6
SEG = 375
SEGP = 384
HUBS = (0, 3, -3, 6, -6)
SECOND = tuple((n, d) for n in range(5) for d in ((-1, 0, 1, 2) if n == 3 else (-1, 0, 1)))
BF = jnp.bfloat16
F32 = jnp.float32
MESH = pl.DeviceIdType.MESH
NT = (((1,), (1,)), ((), ()))


def iota(shape, dim):
    return lax.broadcasted_iota(jnp.int32, shape, dim)


def onehot(mask):
    return jnp.where(mask, 1.0, 0.0).astype(BF)


def kernel(
    v_hbm, c_hbm, pv_hbm, pc_hbm, w_ref, b_ref, out_ref,
    v_ref, c_ref, pv_ref, pc_ref,
    hub, cpad, g_all, swap_out, swap_in, got, low_f32, turned, left, left_e,
    w_all, b_all, w_turned, b_turned, send0, send1, recv0, recv1, panel, seg_out, seg_in, total, y_in,
    loc_sem, wb_ssem, wb_rsem, a_ssem, a_rsem, s_ssem, s_rsem, g_ssem, g_rsem, h_ssem, h_rsem,
    f_ssem, f_rsem, b_ssem, b_rsem, c_ssem, c_rsem, y_ssem, y_rsem,
):
    row = lax.axis_index("prow")
    col = lax.axis_index("pcol")
    z = lax.div(row, 2)
    ylo = lax.rem(row, 2)
    core = lax.rem(col, 2)
    chip = lax.div(col, 2)
    mate = col + 1 - 2 * core
    other_row = row + 1 - 2 * ylo

    def around(i):
        return lax.rem(i + NZ, NZ)

    def remote(src, dst, ssem, rsem, prow, pcol):
        return pltpu.make_async_remote_copy(
            src_ref=src, dst_ref=dst, send_sem=ssem, recv_sem=rsem,
            device_id={"prow": prow, "pcol": pcol}, device_id_type=MESH,
        )

    loads = [
        pltpu.make_async_copy(src, dst, loc_sem.at[n])
        for n, (src, dst) in enumerate(
            ((c_hbm, c_ref), (pc_hbm, pc_ref), (v_hbm, v_ref), (pv_hbm, pv_ref), (w_ref, w_all.at[core]), (b_ref, b_all.at[core]))
        )
    ]
    for copy in loads:
        copy.start()

    barrier = pltpu.get_barrier_semaphore()

    def greet(prow, pcol):
        pl.semaphore_signal(barrier, inc=1, device_id={"prow": prow, "pcol": pcol}, device_id_type=MESH)

    def step_of(plane):
        ahead = around(z - plane)
        back = 1 - lax.rem(17 - ahead, 3)
        return jnp.where(ahead > 8, back, jnp.where(ahead == 8, 2, lax.rem(ahead + 1, 3) - 1))

    hub_z = [around(z - step_of(2 * chip + e)) for e in range(2)]

    for n in (4, 3, 2, 1):
        greet(2 * around(z - HUBS[n]) + ylo, col)
    greet(other_row, col)

    def greet_step(i, _):
        for e in range(2):
            for y in range(2):
                @pl.when((hub_z[e] != z) | (ylo != y) | (i != chip))
                def _(e=e, y=y):
                    greet(2 * hub_z[e] + y, 2 * i + core)

        return 0

    lax.fori_loop(0, 8, greet_step, 0)

    def greet_line(i, _):
        @pl.when(i != col)
        def _():
            greet(row, i)

        return 0

    lax.fori_loop(0, NZ, greet_line, 0)

    for copy in loads[:4]:
        copy.wait()
    val = v_ref[...]
    con = c_ref[...]
    bands = iota((NB, 128), 0)
    lanes = iota((NB, 128), 1)
    vp = jnp.dot(val, onehot(bands == pv_ref[...]), preferred_element_type=F32)
    cp = jnp.dot(con, onehot(bands == pc_ref[...]), preferred_element_type=F32)
    lane = iota((PTS, 128), 1)
    first = jnp.where(lane < 64, cp, pltpu.roll(vp, 64, 1))
    second = jnp.where(lane < 64, pltpu.roll(cp, 64, 1), vp)
    cpad[...] = jnp.zeros((128, NB), BF)
    cpad[pl.ds(pl.multiple_of(lax.rem(col, 4) * PTS, PTS), PTS), :] = con
    low_rows = iota((16, NB), 0)
    low_sel = onehot((low_rows == iota((16, NB), 1)) & (low_rows < NCW))
    low = lax.dot_general(low_sel, cpad[...], NT, preferred_element_type=F32)
    swap_out[0:PTS, :] = jnp.where(core == 0, second, first).astype(BF)
    swap_out[PTS:, :] = low.astype(BF)
    own_pts = pl.ds(pl.multiple_of(core * PTS, PTS), PTS)
    mate_pts = pl.ds(pl.multiple_of((1 - core) * PTS, PTS), PTS)
    hub[0, own_pts, :] = jnp.where(core == 0, first, second).astype(BF)
    tail = jnp.dot(val, onehot((bands == lanes + 896) & (lanes < 104)), preferred_element_type=F32)
    tail = tail + jnp.dot(con, onehot((bands + 104 == lanes) & (bands < NCW)), preferred_element_type=F32)
    g_all[pl.ds(col, 1), :, 0:896] = val[:, 0:896].reshape(1, PTS, 896)
    g_all[pl.ds(col, 1), :, 896:NBP] = tail.astype(BF).reshape(1, PTS, 128)

    pl.semaphore_wait(barrier, 52 - jnp.where((hub_z[0] == z) | (hub_z[1] == z), 1, 0))
    def g_copy(k):
        return remote(g_all.at[col], g_all.at[col], g_ssem.at[k], g_rsem.at[chip], row, 2 * k + core)

    def g_start(i, _):
        there = lax.rem(chip + i, 8)
        g_copy(there).start()
        return 0

    lax.fori_loop(1, 8, g_start, 0)

    def h_copy(k, mine):
        slot = 2 * k + mine
        return remote(g_all.at[slot], g_all.at[slot], h_ssem.at[k], h_rsem.at[k], row, mate)

    h_copy(chip, core).start()

    swap = remote(swap_out, swap_in, f_ssem, f_rsem, row, mate)
    swap.start()
    swap.wait_recv()
    hub[0, mate_pts, :] = swap_in[0:PTS, :]
    hub[0, 2 * PTS :, :] = (low + swap_in[PTS:, :].astype(F32)).astype(BF)

    def s_copy(n):
        return remote(hub.at[0], hub.at[n], s_ssem.at[n], s_rsem.at[n], 2 * around(z + HUBS[n]) + ylo, col)

    for n in (3, 4, 1, 2):
        s_copy(n).start()

    def a_copy(m, y):
        n, d = SECOND[m]
        plane = around(z - HUBS[n])
        return remote(
            hub.at[n], got.at[lax.rem(plane, 2), ylo, chip], a_ssem.at[m, y], a_rsem.at[lax.rem(plane, 2), ylo, chip],
            2 * around(z + d) + y, 2 * lax.div(plane, 2) + core,
        )

    def own_plane(n):
        return lax.div(around(z - HUBS[n]), 2) == chip

    def a_to_self(m, y):
        n, d = SECOND[m]
        return own_plane(n) & (ylo == y) if d == 0 else None

    def a_start(n):
        for m in range(len(SECOND)):
            if SECOND[m][0] == n:
                for y in range(2):
                    own = a_to_self(m, y)
                    if own is None:
                        a_copy(m, y).start()
                    else:
                        @pl.when(jnp.logical_not(own))
                        def _(m=m, y=y):
                            a_copy(m, y).start()

        @pl.when(own_plane(n))
        def _():
            got[lax.rem(around(z - HUBS[n]), 2), ylo, chip] = hub[n]

    a_start(0)

    w_copy = remote(w_ref, w_all.at[core], wb_ssem.at[0], wb_rsem.at[0], row, mate)
    b_copy = remote(b_ref, b_all.at[core], wb_ssem.at[1], wb_rsem.at[1], row, mate)
    w_copy.start()
    b_copy.start()

    for n in (1, 2, 3, 4):
        s_copy(n).wait_recv()
        a_start(n)

    loads[4].wait()
    loads[5].wait()
    w_copy.wait_recv()
    b_copy.wait_recv()

    def turn(i, _):
        e, t = lax.div(i, 4), lax.rem(i, 4)
        span = pl.ds(pl.multiple_of(t * 256, 256), 256)
        rows = pl.ds(pl.multiple_of(e * COLS + t * 256, 256), 256)
        w_turned[rows, :] = w_all[e, :, span].T
        b_turned[rows, :] = b_all[e, :, span].T
        return 0

    lax.fori_loop(0, 8, turn, 0)

    eye = onehot(iota((128, 128), 0) == iota((128, 128), 1))

    def arrive(e, y):
        def a_recv(i, _):
            @pl.when((hub_z[e] != z) | (ylo != y) | (i != chip))
            def _():
                remote(hub.at[0], got.at[e, y, i], a_ssem.at[0, 0], a_rsem.at[e, y, i], row, mate).wait_recv()

            return 0

        lax.fori_loop(0, 8, a_recv, 0)

    for e in range(2):
        for y in range(2):
            arrive(e, y)

    for e in range(2):
        for y in range(2):
            at = (2 * e + y) * ROWS
            rows = got[e, y, :, 0:64, :].reshape(ROWS, 128)
            turned[:, at : at + ROWS] = lax.dot_general(eye, rows, NT, preferred_element_type=F32)
            for g in range(4):
                low_f32[:, at + g * 128 : at + g * 128 + 128] = (
                    got[e, y, 2 * g, 64:80, :].astype(F32) + got[e, y, 2 * g + 1, 64:80, :].astype(F32)
                )

    left_e[...] = (turned[0:64, :] * turned[64:128, :]).astype(BF)

    def against(lhs, rhs, span):
        return jnp.dot(lhs[...], rhs[:, span], preferred_element_type=F32)

    def band_of(parity, i):
        return 3 * parity + i + 3 * (i // 3)

    def plane_of(parity, i):
        return 4 * parity + i + 4 * lax.div(i, 4)

    near = lax.rem(lax.div(z, 4), 2)

    def build(parity):
        def step(m, _):
            tile = turned[pl.ds(pl.multiple_of(m * 8, 8), 8), :]
            for p in range(HALF // 2):
                pair = jnp.concatenate(
                    [tile * low_f32[pl.ds(band_of(parity, 2 * p + k), 1), :] for k in range(2)], axis=0
                )
                left[pl.ds(pl.multiple_of(m * 48 + 16 * p, 16), 16), :] = pair.astype(BF)
            return 0

        lax.fori_loop(0, 8, step, 0)

    def b_copy_to(n, m):
        sends, recvs = ((send0, recv0), (send1, recv1))[n]
        return remote(sends.at[m], recvs.at[chip], b_ssem.at[n, m], b_rsem.at[n, chip], row, 8 * core + m)

    order = (near, 1 - near)
    for n in range(2):
        sends, recvs = ((send0, recv0), (send1, recv1))[n]
        build(order[n])

        def mul(t, _, n=n, sends=sends):
            span = pl.ds(pl.multiple_of(t * 256, 256), 256)
            d = against(left, w_turned, span).astype(BF)
            for m in range(8):
                sends[m, 0:48, span] = d[m * 48 : (m + 1) * 48, :]
            if n == 0:
                e = against(left_e, b_turned, span)
                head = e.astype(BF).astype(F32)
                rest = e - head
                for m in range(8):
                    both = jnp.concatenate([head[m * 8 : m * 8 + 8], rest[m * 8 : m * 8 + 8]], axis=0)
                    sends[m, 48:64, span] = both.astype(BF)
            return 0

        lax.fori_loop(0, 2, mul, 0)

        def b_start(m, _, n=n, sends=sends, recvs=recvs):
            @pl.when(8 * core + m != col)
            def _():
                b_copy_to(n, m).start()

            @pl.when(8 * core + m == col)
            def _():
                recvs[pl.ds(chip, 1)] = sends[pl.ds(m, 1)]

            return 0

        lax.fori_loop(0, 8, b_start, 0)

    def h_start(i, _):
        k = lax.rem(chip + i, 8)
        remote(g_all.at[col], g_all.at[2 * k + core], g_ssem.at[k], g_rsem.at[k], row, mate).wait_recv()
        h_copy(k, core).start()
        return 0

    lax.fori_loop(1, 8, h_start, 0)

    def h_wait(i, _):
        h_copy(i, 1 - core).wait_recv()
        return 0

    lax.fori_loop(0, 8, h_wait, 0)
    points = g_all[...].reshape(ROWS, NBP)
    mine = jnp.where(iota((8, 128), 1) == col * 8 + iota((8, 128), 0), pv_ref[...].astype(F32), 0.0)
    sel = onehot(jnp.sum(mine, axis=1, keepdims=True) == iota((8, NBP), 1).astype(F32))
    vpt = lax.dot_general(sel, points, NT, preferred_element_type=F32)
    sel = onehot((iota((16, NBP), 1) == iota((16, NBP), 0) + NB) & (iota((16, NBP), 0) < NCW))
    low_f32[:, 0:ROWS] = lax.dot_general(sel, points, NT, preferred_element_type=F32)

    def b_recv(n):
        recvs = (recv0, recv1)[n]

        def step(k, _):
            @pl.when(2 * k + lax.div(col, 8) != col)
            def _():
                remote(recvs.at[k], recvs.at[k], b_ssem.at[n, 0], b_rsem.at[n, k], row, mate).wait_recv()

            return 0

        lax.fori_loop(0, 8, step, 0)

    def c_copy(i):
        return remote(seg_out.at[i], seg_in.at[z], c_ssem.at[i], c_rsem.at[z], 2 * i + ylo, col)

    lane = iota((8, SEGP), 1)
    for n in range(2):
        recvs = (recv0, recv1)[n]
        parity = order[n]
        b_recv(n)
        d = recvs[0].astype(F32)
        for k in range(1, 8):
            d = d + recvs[k].astype(F32)
        if n == 0:
            exch = 2.0 * (d[48:56] + d[56:64])
        comb = [
            low_f32[pl.ds(band_of(parity, i), 1), 0:ROWS] * exch - vpt * d[i * 8 : i * 8 + 8] for i in range(HALF)
        ]
        comb = jnp.concatenate(comb, axis=0).astype(BF)
        panel[...] = jnp.dot(comb, points, preferred_element_type=F32)
        for zl in range(8):
            halves = []
            for y in range(2):
                start = SEG * (2 * zl + y)
                band0, off = start // NB, start % NB
                seg = panel[band0 * 8 : band0 * 8 + 8, :]
                if off:
                    seg = pltpu.roll(seg, NBP - off, 1)
                seg = seg[:, 0:SEGP]
                if off + SEG > NB:
                    more = pltpu.roll(panel[band0 * 8 + 8 : band0 * 8 + 16, :], NB - off, 1)[:, 0:SEGP]
                    seg = jnp.where(lane < NB - off, seg, more)
                halves.append(seg)
            seg_out[pl.ds(plane_of(parity, zl), 1)] = jnp.concatenate(halves, axis=0).astype(BF).reshape(1, 16, SEGP)

        def c_start(i, _, parity=parity):
            there = plane_of(parity, i)

            @pl.when(there != z)
            def _():
                c_copy(there).start()

            @pl.when(there == z)
            def _():
                seg_in[pl.ds(z, 1)] = seg_out[pl.ds(z, 1)]

            return 0

        lax.fori_loop(0, 8, c_start, 0)

    def c_recv(i, _):
        @pl.when(i != z)
        def _():
            remote(seg_out.at[i], seg_in.at[i], c_ssem.at[i], c_rsem.at[i], row, mate).wait_recv()

        return 0

    lax.fori_loop(0, NZ, c_recv, 0)
    acc = seg_in[0].astype(F32)
    for i in range(1, NZ):
        acc = acc + seg_in[i].astype(F32)
    total[...] = acc.reshape(2, 8, SEGP)
    y_copy = remote(total.at[1 - ylo], y_in, y_ssem, y_rsem, other_row, col)
    y_copy.start()

    def drain(i, _):
        @pl.when(i != z)
        def _():
            c_copy(i).wait_send()

        return 0

    lax.fori_loop(0, NZ, drain, 0)
    for n in range(1, 5):
        s_copy(n).wait_send()
    for m in range(len(SECOND)):
        for y in range(2):
            own = a_to_self(m, y)
            if own is None:
                a_copy(m, y).wait_send()
            else:
                @pl.when(jnp.logical_not(own))
                def _(m=m, y=y):
                    a_copy(m, y).wait_send()

    def drain8(i, _):
        @pl.when(i != chip)
        def _():
            g_copy(i).wait_send()

        h_copy(i, core).wait_send()

        @pl.when(8 * core + i != col)
        def _():
            b_copy_to(0, i).wait_send()
            b_copy_to(1, i).wait_send()

        return 0

    lax.fori_loop(0, 8, drain8, 0)
    swap.wait_send()
    w_copy.wait_send()
    b_copy.wait_send()
    y_copy.wait()
    out_ref[...] = total[ylo] + y_in[...]


def body(orb_valence, orb_conduction, screened, bare, panel_valence, panel_conduction):
    vmem = pl.BlockSpec(memory_space=pltpu.VMEM)
    hbm = pl.BlockSpec(memory_space=pl.ANY)
    dma = pltpu.SemaphoreType.DMA
    out = pl.pallas_call(
        kernel,
        out_shape=jax.ShapeDtypeStruct((8, SEGP), F32),
        in_specs=[hbm] * 6,
        out_specs=vmem,
        scratch_shapes=[
            pltpu.VMEM((PTS, NB), BF),
            pltpu.VMEM((PTS, NB), BF),
            pltpu.VMEM((1, 128), jnp.int32),
            pltpu.VMEM((1, 128), jnp.int32),
            pltpu.VMEM((5, 80, 128), BF),
            pltpu.VMEM((128, NB), BF),
            pltpu.VMEM((NCOL, PTS, NBP), BF),
            pltpu.VMEM((48, 128), BF),
            pltpu.VMEM((48, 128), BF),
            pltpu.VMEM((2, 2, 8, 80, 128), BF),
            pltpu.VMEM((16, 2 * COLS), F32),
            pltpu.VMEM((128, 2 * COLS), F32),
            pltpu.VMEM((8 * HALF * 8, 2 * COLS), BF),
            pltpu.VMEM((64, 2 * COLS), BF),
            pltpu.VMEM((2, ROWS, COLS), BF),
            pltpu.VMEM((2, ROWS, COLS), BF),
            pltpu.VMEM((2 * COLS, ROWS), BF),
            pltpu.VMEM((2 * COLS, ROWS), BF),
            pltpu.VMEM((8, 64, ROWS), BF),
            pltpu.VMEM((8, 48, ROWS), BF),
            pltpu.VMEM((8, 64, ROWS), BF),
            pltpu.VMEM((8, 48, ROWS), BF),
            pltpu.VMEM((48, NBP), F32),
            pltpu.VMEM((NZ, 16, SEGP), BF),
            pltpu.VMEM((NZ, 16, SEGP), BF),
            pltpu.VMEM((2, 8, SEGP), F32),
            pltpu.VMEM((8, SEGP), F32),
            dma((6,)),
            dma((2,)), dma((2,)),
            dma((len(SECOND), 2)), dma((2, 2, 8)),
            dma((5,)), dma((5,)),
            dma((8,)), dma((8,)),
            dma((8,)), dma((8,)),
            dma, dma,
            dma((2, 8)), dma((2, 8)),
            dma((16,)), dma((16,)),
            dma, dma,
        ],
        compiler_params=pltpu.CompilerParams(
            collective_id=0, has_side_effects=True, vmem_limit_bytes=60 * 2**20
        ),
        name="kernel_panel",
    )(
        orb_valence, orb_conduction, panel_valence.reshape(1, -1), panel_conduction.reshape(1, -1),
        screened, bare,
    )
    return out[:, :SEG].T


def solution(mesh):
    placed = (
        P(("prow", "pcol"), None),
        P(("prow", "pcol"), None),
        P("prow", "pcol"),
        P("prow", "pcol"),
        P(),
        P(),
    )
    return jax.shard_map(
        body, mesh=mesh, in_specs=placed, out_specs=P("prow", "pcol"), check_vma=False
    )
```

```python
import jax
import jax.numpy as jnp
from jax import lax
from jax.experimental import pallas as pl
from jax.experimental.pallas import tpu as pltpu
from jax.sharding import PartitionSpec as P

NCW = 12
NZ = 16
NCOL = 16
PTS = 32
ROWS = PTS * NCOL
COLS = 1024
NB = 1000
NBP = 1024
QUARTERS = ((2,), (1, 3), (0,))
SENT = (32, 48, 32)
SEG = 375
SEGP = 384
HUBS = (0, 3, -3, 6, -6)
SECOND = tuple((n, d) for n in range(5) for d in ((-1, 0, 1, 2) if n == 3 else (-1, 0, 1)))
BF = jnp.bfloat16
F32 = jnp.float32
MESH = pl.DeviceIdType.MESH
NT = (((1,), (1,)), ((), ()))


def iota(shape, dim):
    return lax.broadcasted_iota(jnp.int32, shape, dim)


def onehot(mask):
    return jnp.where(mask, 1.0, 0.0).astype(BF)


def kernel(
    v_hbm, c_hbm, pv_hbm, pc_hbm, w_ref, b_ref, out_ref,
    v_ref, c_ref, pv_ref, pc_ref,
    hub, cpad, g_all, swap_out, swap_in, got, low_f32, turned, left, left_e,
    w_all, b_all, w_turned, b_turned, send0, send1, send2, recv0, recv1, recv2, panel, seg_out, seg_in, total, y_in,
    loc_sem, wb_ssem, wb_rsem, a_ssem, a_rsem, s_ssem, s_rsem, g_ssem, g_rsem, h_ssem, h_rsem,
    f_ssem, f_rsem, b_ssem, b_rsem, c_ssem, c_rsem, y_ssem, y_rsem,
):
    row = lax.axis_index("prow")
    col = lax.axis_index("pcol")
    z = lax.div(row, 2)
    ylo = lax.rem(row, 2)
    core = lax.rem(col, 2)
    chip = lax.div(col, 2)
    mate = col + 1 - 2 * core
    other_row = row + 1 - 2 * ylo

    def around(i):
        return lax.rem(i + NZ, NZ)

    def remote(src, dst, ssem, rsem, prow, pcol):
        return pltpu.make_async_remote_copy(
            src_ref=src, dst_ref=dst, send_sem=ssem, recv_sem=rsem,
            device_id={"prow": prow, "pcol": pcol}, device_id_type=MESH,
        )

    loads = [
        pltpu.make_async_copy(src, dst, loc_sem.at[n])
        for n, (src, dst) in enumerate(
            ((c_hbm, c_ref), (pc_hbm, pc_ref), (v_hbm, v_ref), (pv_hbm, pv_ref), (w_ref, w_all.at[core]), (b_ref, b_all.at[core]))
        )
    ]
    for copy in loads:
        copy.start()

    barrier = pltpu.get_barrier_semaphore()

    def greet(prow, pcol):
        pl.semaphore_signal(barrier, inc=1, device_id={"prow": prow, "pcol": pcol}, device_id_type=MESH)

    def step_of(plane):
        ahead = around(z - plane)
        back = 1 - lax.rem(17 - ahead, 3)
        return jnp.where(ahead > 8, back, jnp.where(ahead == 8, 2, lax.rem(ahead + 1, 3) - 1))

    hub_z = [around(z - step_of(2 * chip + e)) for e in range(2)]

    for n in (4, 3, 2, 1):
        greet(2 * around(z - HUBS[n]) + ylo, col)
    greet(other_row, col)

    def greet_step(i, _):
        for e in range(2):
            for y in range(2):
                @pl.when((hub_z[e] != z) | (ylo != y) | (i != chip))
                def _(e=e, y=y):
                    greet(2 * hub_z[e] + y, 2 * i + core)

        return 0

    lax.fori_loop(0, 8, greet_step, 0)

    def greet_line(i, _):
        @pl.when(i != col)
        def _():
            greet(row, i)

        return 0

    lax.fori_loop(0, NZ, greet_line, 0)

    for copy in loads[:4]:
        copy.wait()
    val = v_ref[...]
    con = c_ref[...]
    bands = iota((NB, 128), 0)
    lanes = iota((NB, 128), 1)
    vp = jnp.dot(val, onehot(bands == pv_ref[...]), preferred_element_type=F32)
    cp = jnp.dot(con, onehot(bands == pc_ref[...]), preferred_element_type=F32)
    lane = iota((PTS, 128), 1)
    first = jnp.where(lane < 64, cp, pltpu.roll(vp, 64, 1))
    second = jnp.where(lane < 64, pltpu.roll(cp, 64, 1), vp)
    cpad[...] = jnp.zeros((128, NB), BF)
    cpad[pl.ds(pl.multiple_of(lax.rem(col, 4) * PTS, PTS), PTS), :] = con
    low_rows = iota((16, NB), 0)
    low_sel = onehot((low_rows == iota((16, NB), 1)) & (low_rows < NCW))
    low = lax.dot_general(low_sel, cpad[...], NT, preferred_element_type=F32)
    swap_out[0:PTS, :] = jnp.where(core == 0, second, first).astype(BF)
    swap_out[PTS:, :] = low.astype(BF)
    own_pts = pl.ds(pl.multiple_of(core * PTS, PTS), PTS)
    mate_pts = pl.ds(pl.multiple_of((1 - core) * PTS, PTS), PTS)
    hub[0, own_pts, :] = jnp.where(core == 0, first, second).astype(BF)
    tail = jnp.dot(val, onehot((bands == lanes + 896) & (lanes < 104)), preferred_element_type=F32)
    tail = tail + jnp.dot(con, onehot((bands + 104 == lanes) & (bands < NCW)), preferred_element_type=F32)
    g_all[pl.ds(col, 1), :, 0:896] = val[:, 0:896].reshape(1, PTS, 896)
    g_all[pl.ds(col, 1), :, 896:NBP] = tail.astype(BF).reshape(1, PTS, 128)

    pl.semaphore_wait(barrier, 52 - jnp.where((hub_z[0] == z) | (hub_z[1] == z), 1, 0))
    def g_copy(k):
        return remote(g_all.at[col], g_all.at[col], g_ssem.at[k], g_rsem.at[chip], row, 2 * k + core)

    def g_start(i, _):
        there = lax.rem(chip + i, 8)
        g_copy(there).start()
        return 0

    lax.fori_loop(1, 8, g_start, 0)

    def h_copy(k, mine):
        slot = 2 * k + mine
        return remote(g_all.at[slot], g_all.at[slot], h_ssem.at[k], h_rsem.at[k], row, mate)

    h_copy(chip, core).start()

    swap = remote(swap_out, swap_in, f_ssem, f_rsem, row, mate)
    swap.start()
    swap.wait_recv()
    hub[0, mate_pts, :] = swap_in[0:PTS, :]
    hub[0, 2 * PTS :, :] = (low + swap_in[PTS:, :].astype(F32)).astype(BF)

    def s_copy(n):
        return remote(hub.at[0], hub.at[n], s_ssem.at[n], s_rsem.at[n], 2 * around(z + HUBS[n]) + ylo, col)

    for n in (3, 4, 1, 2):
        s_copy(n).start()

    def a_copy(m, y):
        n, d = SECOND[m]
        plane = around(z - HUBS[n])
        return remote(
            hub.at[n], got.at[lax.rem(plane, 2), ylo, chip], a_ssem.at[m, y], a_rsem.at[lax.rem(plane, 2), ylo, chip],
            2 * around(z + d) + y, 2 * lax.div(plane, 2) + core,
        )

    def own_plane(n):
        return lax.div(around(z - HUBS[n]), 2) == chip

    def a_to_self(m, y):
        n, d = SECOND[m]
        return own_plane(n) & (ylo == y) if d == 0 else None

    def a_start(n):
        for m in range(len(SECOND)):
            if SECOND[m][0] == n:
                for y in range(2):
                    own = a_to_self(m, y)
                    if own is None:
                        a_copy(m, y).start()
                    else:
                        @pl.when(jnp.logical_not(own))
                        def _(m=m, y=y):
                            a_copy(m, y).start()

        @pl.when(own_plane(n))
        def _():
            got[lax.rem(around(z - HUBS[n]), 2), ylo, chip] = hub[n]

    a_start(0)

    w_copy = remote(w_ref, w_all.at[core], wb_ssem.at[0], wb_rsem.at[0], row, mate)
    b_copy = remote(b_ref, b_all.at[core], wb_ssem.at[1], wb_rsem.at[1], row, mate)
    w_copy.start()
    b_copy.start()

    for n in (1, 2, 3, 4):
        s_copy(n).wait_recv()
        a_start(n)

    loads[4].wait()
    loads[5].wait()
    w_copy.wait_recv()
    b_copy.wait_recv()

    def turn(i, _):
        e, t = lax.div(i, 4), lax.rem(i, 4)
        span = pl.ds(pl.multiple_of(t * 256, 256), 256)
        rows = pl.ds(pl.multiple_of(e * COLS + t * 256, 256), 256)
        w_turned[rows, :] = w_all[e, :, span].T
        b_turned[rows, :] = b_all[e, :, span].T
        return 0

    lax.fori_loop(0, 8, turn, 0)

    eye = onehot(iota((128, 128), 0) == iota((128, 128), 1))

    def arrive(e, y):
        def a_recv(i, _):
            @pl.when((hub_z[e] != z) | (ylo != y) | (i != chip))
            def _():
                remote(hub.at[0], got.at[e, y, i], a_ssem.at[0, 0], a_rsem.at[e, y, i], row, mate).wait_recv()

            return 0

        lax.fori_loop(0, 8, a_recv, 0)

    for e in range(2):
        for y in range(2):
            arrive(e, y)

    for e in range(2):
        for y in range(2):
            at = (2 * e + y) * ROWS
            rows = got[e, y, :, 0:64, :].reshape(ROWS, 128)
            turned[:, at : at + ROWS] = lax.dot_general(eye, rows, NT, preferred_element_type=F32)
            for g in range(4):
                low_f32[:, at + g * 128 : at + g * 128 + 128] = (
                    got[e, y, 2 * g, 64:80, :].astype(F32) + got[e, y, 2 * g + 1, 64:80, :].astype(F32)
                )

    left_e[...] = (turned[0:64, :] * turned[64:128, :]).astype(BF)

    def place(n, i, size):
        quarter = lax.rem(lax.div(z, 4) + QUARTERS[n][0] + 2 * lax.div(i, size), 4)
        return quarter * size + lax.rem(i, size)

    def build(n):
        bands_here = 3 * len(QUARTERS[n])

        def step(m, _):
            tile = turned[pl.ds(pl.multiple_of(m * 8, 8), 8), :]
            for p in range(SENT[n] // 16):
                pair = [
                    tile * low_f32[pl.ds(place(n, i, 3), 1), :] if i < bands_here else jnp.zeros_like(tile)
                    for i in (2 * p, 2 * p + 1)
                ]
                rows = pl.ds(pl.multiple_of(m * SENT[n] + 16 * p, 16), 16)
                left[rows, :] = jnp.concatenate(pair, axis=0).astype(BF)
            return 0

        lax.fori_loop(0, 8, step, 0)

    buffers = ((send0, recv0), (send1, recv1), (send2, recv2))

    def b_copy_to(n, m):
        sends, recvs = buffers[n]
        return remote(sends.at[m], recvs.at[chip], b_ssem.at[n, m], b_rsem.at[n, chip], row, 8 * core + m)

    for n in range(3):
        sends, recvs = buffers[n]
        build(n)

        def mul(t, _, n=n, sends=sends):
            span = pl.ds(pl.multiple_of(t * 256, 256), 256)
            size = SENT[n]
            d = jnp.dot(left[0 : 8 * size, :], w_turned[:, span], preferred_element_type=F32)
            if n == 0:
                e = jnp.dot(left_e[...], b_turned[:, span], preferred_element_type=F32)
                for m in range(8):
                    both = jnp.concatenate([d[m * size : m * size + 24], e[m * 8 : m * 8 + 8]], axis=0)
                    sends[m, :, span] = both.astype(BF)
            else:
                d = d.astype(BF)
                for m in range(8):
                    sends[m, :, span] = d[m * size : (m + 1) * size, :]
            return 0

        lax.fori_loop(0, 2, mul, 0)

        def b_start(m, _, n=n, sends=sends, recvs=recvs):
            @pl.when(8 * core + m != col)
            def _():
                b_copy_to(n, m).start()

            @pl.when(8 * core + m == col)
            def _():
                recvs[pl.ds(chip, 1)] = sends[pl.ds(m, 1)]

            return 0

        lax.fori_loop(0, 8, b_start, 0)

    def h_start(i, _):
        k = lax.rem(chip + i, 8)
        remote(g_all.at[col], g_all.at[2 * k + core], g_ssem.at[k], g_rsem.at[k], row, mate).wait_recv()
        h_copy(k, core).start()
        return 0

    lax.fori_loop(1, 8, h_start, 0)

    def h_wait(i, _):
        h_copy(i, 1 - core).wait_recv()
        return 0

    lax.fori_loop(0, 8, h_wait, 0)
    points = g_all[...].reshape(ROWS, NBP)
    mine = jnp.where(iota((8, 128), 1) == col * 8 + iota((8, 128), 0), pv_ref[...].astype(F32), 0.0)
    sel = onehot(jnp.sum(mine, axis=1, keepdims=True) == iota((8, NBP), 1).astype(F32))
    vpt = lax.dot_general(sel, points, NT, preferred_element_type=F32)
    sel = onehot((iota((16, NBP), 1) == iota((16, NBP), 0) + NB) & (iota((16, NBP), 0) < NCW))
    low_f32[:, 0:ROWS] = lax.dot_general(sel, points, NT, preferred_element_type=F32)

    def b_recv(n):
        recvs = buffers[n][1]

        def step(k, _):
            @pl.when(2 * k + lax.div(col, 8) != col)
            def _():
                remote(recvs.at[k], recvs.at[k], b_ssem.at[n, 0], b_rsem.at[n, k], row, mate).wait_recv()

            return 0

        lax.fori_loop(0, 8, step, 0)

    def c_copy(i):
        return remote(seg_out.at[i], seg_in.at[z], c_ssem.at[i], c_rsem.at[z], 2 * i + ylo, col)

    lane = iota((8, SEGP), 1)
    for n in range(3):
        recvs = buffers[n][1]
        count = 3 * len(QUARTERS[n])
        b_recv(n)
        d = recvs[0].astype(F32)
        for k in range(1, 8):
            d = d + recvs[k].astype(F32)
        if n == 0:
            exch = 2.0 * d[24:32]
        comb = [
            low_f32[pl.ds(place(n, i, 3), 1), 0:ROWS] * exch - vpt * d[i * 8 : i * 8 + 8] for i in range(count)
        ]
        if count == 3:
            comb.append(jnp.zeros_like(exch))
        comb = jnp.concatenate(comb, axis=0).astype(BF)
        panel[0 : SENT[n], :] = jnp.dot(comb, points, preferred_element_type=F32)
        for zl in range(4 * len(QUARTERS[n])):
            halves = []
            for y in range(2):
                start = SEG * (2 * zl + y)
                band0, off = start // NB, start % NB
                seg = panel[band0 * 8 : band0 * 8 + 8, :]
                if off:
                    seg = pltpu.roll(seg, NBP - off, 1)
                seg = seg[:, 0:SEGP]
                if off + SEG > NB:
                    more = pltpu.roll(panel[band0 * 8 + 8 : band0 * 8 + 16, :], NB - off, 1)[:, 0:SEGP]
                    seg = jnp.where(lane < NB - off, seg, more)
                halves.append(seg)
            seg_out[pl.ds(place(n, jnp.int32(zl), 4), 1)] = jnp.concatenate(halves, axis=0).astype(BF).reshape(1, 16, SEGP)

        def c_start(i, _, n=n):
            there = place(n, i, 4)

            @pl.when(there != z)
            def _():
                c_copy(there).start()

            @pl.when(there == z)
            def _():
                seg_in[pl.ds(z, 1)] = seg_out[pl.ds(z, 1)]

            return 0

        lax.fori_loop(0, 4 * len(QUARTERS[n]), c_start, 0)

    def c_recv(i, _):
        @pl.when(i != z)
        def _():
            remote(seg_out.at[i], seg_in.at[i], c_ssem.at[i], c_rsem.at[i], row, mate).wait_recv()

        return 0

    lax.fori_loop(0, NZ, c_recv, 0)
    acc = seg_in[0].astype(F32)
    for i in range(1, NZ):
        acc = acc + seg_in[i].astype(F32)
    total[...] = acc.reshape(2, 8, SEGP)
    y_copy = remote(total.at[1 - ylo], y_in, y_ssem, y_rsem, other_row, col)
    y_copy.start()

    def drain(i, _):
        @pl.when(i != z)
        def _():
            c_copy(i).wait_send()

        return 0

    lax.fori_loop(0, NZ, drain, 0)
    for n in range(1, 5):
        s_copy(n).wait_send()
    for m in range(len(SECOND)):
        for y in range(2):
            own = a_to_self(m, y)
            if own is None:
                a_copy(m, y).wait_send()
            else:
                @pl.when(jnp.logical_not(own))
                def _(m=m, y=y):
                    a_copy(m, y).wait_send()

    def drain8(i, _):
        @pl.when(i != chip)
        def _():
            g_copy(i).wait_send()

        h_copy(i, core).wait_send()

        @pl.when(8 * core + i != col)
        def _():
            for n in range(3):
                b_copy_to(n, i).wait_send()

        return 0

    lax.fori_loop(0, 8, drain8, 0)
    swap.wait_send()
    w_copy.wait_send()
    b_copy.wait_send()
    y_copy.wait()
    out_ref[...] = total[ylo] + y_in[...]


def body(orb_valence, orb_conduction, screened, bare, panel_valence, panel_conduction):
    vmem = pl.BlockSpec(memory_space=pltpu.VMEM)
    hbm = pl.BlockSpec(memory_space=pl.ANY)
    dma = pltpu.SemaphoreType.DMA
    out = pl.pallas_call(
        kernel,
        out_shape=jax.ShapeDtypeStruct((8, SEGP), F32),
        in_specs=[hbm] * 6,
        out_specs=vmem,
        scratch_shapes=[
            pltpu.VMEM((PTS, NB), BF),
            pltpu.VMEM((PTS, NB), BF),
            pltpu.VMEM((1, 128), jnp.int32),
            pltpu.VMEM((1, 128), jnp.int32),
            pltpu.VMEM((5, 80, 128), BF),
            pltpu.VMEM((128, NB), BF),
            pltpu.VMEM((NCOL, PTS, NBP), BF),
            pltpu.VMEM((48, 128), BF),
            pltpu.VMEM((48, 128), BF),
            pltpu.VMEM((2, 2, 8, 80, 128), BF),
            pltpu.VMEM((16, 2 * COLS), F32),
            pltpu.VMEM((128, 2 * COLS), F32),
            pltpu.VMEM((8 * 48, 2 * COLS), BF),
            pltpu.VMEM((64, 2 * COLS), BF),
            pltpu.VMEM((2, ROWS, COLS), BF),
            pltpu.VMEM((2, ROWS, COLS), BF),
            pltpu.VMEM((2 * COLS, ROWS), BF),
            pltpu.VMEM((2 * COLS, ROWS), BF),
            pltpu.VMEM((8, 32, ROWS), BF),
            pltpu.VMEM((8, 48, ROWS), BF),
            pltpu.VMEM((8, 32, ROWS), BF),
            pltpu.VMEM((8, 32, ROWS), BF),
            pltpu.VMEM((8, 48, ROWS), BF),
            pltpu.VMEM((8, 32, ROWS), BF),
            pltpu.VMEM((48, NBP), F32),
            pltpu.VMEM((NZ, 16, SEGP), BF),
            pltpu.VMEM((NZ, 16, SEGP), BF),
            pltpu.VMEM((2, 8, SEGP), F32),
            pltpu.VMEM((8, SEGP), F32),
            dma((6,)),
            dma((2,)), dma((2,)),
            dma((len(SECOND), 2)), dma((2, 2, 8)),
            dma((5,)), dma((5,)),
            dma((8,)), dma((8,)),
            dma((8,)), dma((8,)),
            dma, dma,
            dma((3, 8)), dma((3, 8)),
            dma((16,)), dma((16,)),
            dma, dma,
        ],
        compiler_params=pltpu.CompilerParams(
            collective_id=0, has_side_effects=True, vmem_limit_bytes=60 * 2**20
        ),
        name="kernel_panel",
    )(
        orb_valence, orb_conduction, panel_valence.reshape(1, -1), panel_conduction.reshape(1, -1),
        screened, bare,
    )
    return out[:, :SEG].T


def solution(mesh):
    placed = (
        P(("prow", "pcol"), None),
        P(("prow", "pcol"), None),
        P("prow", "pcol"),
        P("prow", "pcol"),
        P(),
        P(),
    )
    return jax.shard_map(
        body, mesh=mesh, in_specs=placed, out_specs=P("prow", "pcol"), check_vma=False
    )
```

```python
import jax
import jax.numpy as jnp
from jax import lax
from jax.experimental import pallas as pl
from jax.experimental.pallas import tpu as pltpu
from jax.sharding import PartitionSpec as P

NCW = 12
NZ = 16
NCOL = 16
PTS = 32
ROWS = PTS * NCOL
COLS = 1024
NB = 1000
NBP = 1024
QUARTERS = ((2,), (1, 3), (0,))
SENT = (32, 48, 32)
SEG = 375
SEGP = 384
HUBS = (0, 3, -3, 6, -6)
SECOND = tuple((n, d) for n in range(5) for d in ((-1, 0, 1, 2) if n == 3 else (-1, 0, 1)))
BF = jnp.bfloat16
F32 = jnp.float32
MESH = pl.DeviceIdType.MESH
NT = (((1,), (1,)), ((), ()))


def iota(shape, dim):
    return lax.broadcasted_iota(jnp.int32, shape, dim)


def onehot(mask):
    return jnp.where(mask, 1.0, 0.0).astype(BF)


def kernel(
    v_hbm, c_hbm, pv_hbm, pc_hbm, w_ref, b_ref, out_ref,
    v_ref, c_ref, pv_ref, pc_ref,
    hub, cpad, g_all, swap_out, swap_in, got, low_f32, turned, left, left_e,
    w_all, b_all, w_turned, b_turned, send0, send1, send2, recv0, recv1, recv2, panel, seg_out, seg_in, total, y_in,
    loc_sem, wb_ssem, wb_rsem, a_ssem, a_rsem, s_ssem, s_rsem, g_ssem, g_rsem, h_ssem, h_rsem,
    f_ssem, f_rsem, b_ssem, b_rsem, c_ssem, c_rsem, y_ssem, y_rsem,
):
    row = lax.axis_index("prow")
    col = lax.axis_index("pcol")
    z = lax.div(row, 2)
    ylo = lax.rem(row, 2)
    core = lax.rem(col, 2)
    chip = lax.div(col, 2)
    mate = col + 1 - 2 * core
    other_row = row + 1 - 2 * ylo

    def around(i):
        return lax.rem(i + NZ, NZ)

    def remote(src, dst, ssem, rsem, prow, pcol):
        return pltpu.make_async_remote_copy(
            src_ref=src, dst_ref=dst, send_sem=ssem, recv_sem=rsem,
            device_id={"prow": prow, "pcol": pcol}, device_id_type=MESH,
        )

    loads = [
        pltpu.make_async_copy(src, dst, loc_sem.at[n])
        for n, (src, dst) in enumerate(
            ((c_hbm, c_ref), (pc_hbm, pc_ref), (v_hbm, v_ref), (pv_hbm, pv_ref), (w_ref, w_all.at[core]), (b_ref, b_all.at[core]))
        )
    ]
    for copy in loads:
        copy.start()

    barrier = pltpu.get_barrier_semaphore()

    def greet(prow, pcol):
        pl.semaphore_signal(barrier, inc=1, device_id={"prow": prow, "pcol": pcol}, device_id_type=MESH)

    def step_of(plane):
        ahead = around(z - plane)
        back = 1 - lax.rem(17 - ahead, 3)
        return jnp.where(ahead > 8, back, jnp.where(ahead == 8, 2, lax.rem(ahead + 1, 3) - 1))

    hub_z = [around(z - step_of(2 * chip + e)) for e in range(2)]

    for n in (4, 3, 2, 1):
        greet(2 * around(z - HUBS[n]) + ylo, col)
    greet(other_row, col)

    def greet_step(i, _):
        for e in range(2):
            for y in range(2):
                @pl.when((hub_z[e] != z) | (ylo != y) | (i != chip))
                def _(e=e, y=y):
                    greet(2 * hub_z[e] + y, 2 * i + core)

        return 0

    lax.fori_loop(0, 8, greet_step, 0)

    def greet_line(i, _):
        @pl.when(i != col)
        def _():
            greet(row, i)

        return 0

    lax.fori_loop(0, NZ, greet_line, 0)

    for copy in loads[:4]:
        copy.wait()
    val = v_ref[...]
    con = c_ref[...]
    bands = iota((NB, 128), 0)
    lanes = iota((NB, 128), 1)
    vp = jnp.dot(val, onehot(bands == pv_ref[...]), preferred_element_type=F32)
    cp = jnp.dot(con, onehot(bands == pc_ref[...]), preferred_element_type=F32)
    lane = iota((PTS, 128), 1)
    first = jnp.where(lane < 64, cp, pltpu.roll(vp, 64, 1))
    second = jnp.where(lane < 64, pltpu.roll(cp, 64, 1), vp)
    cpad[...] = jnp.zeros((128, NB), BF)
    cpad[pl.ds(pl.multiple_of(lax.rem(col, 4) * PTS, PTS), PTS), :] = con
    low_rows = iota((16, NB), 0)
    low_sel = onehot((low_rows == iota((16, NB), 1)) & (low_rows < NCW))
    low = lax.dot_general(low_sel, cpad[...], NT, preferred_element_type=F32)
    swap_out[0:PTS, :] = jnp.where(core == 0, second, first).astype(BF)
    swap_out[PTS:, :] = low.astype(BF)
    own_pts = pl.ds(pl.multiple_of(core * PTS, PTS), PTS)
    mate_pts = pl.ds(pl.multiple_of((1 - core) * PTS, PTS), PTS)
    hub[0, own_pts, :] = jnp.where(core == 0, first, second).astype(BF)
    tail = jnp.dot(val, onehot((bands == lanes + 896) & (lanes < 104)), preferred_element_type=F32)
    tail = tail + jnp.dot(con, onehot((bands + 104 == lanes) & (bands < NCW)), preferred_element_type=F32)
    g_all[pl.ds(col, 1), :, 0:896] = val[:, 0:896].reshape(1, PTS, 896)
    g_all[pl.ds(col, 1), :, 896:NBP] = tail.astype(BF).reshape(1, PTS, 128)

    pl.semaphore_wait(barrier, 52 - jnp.where((hub_z[0] == z) | (hub_z[1] == z), 1, 0))
    def g_copy(k):
        return remote(g_all.at[col], g_all.at[col], g_ssem.at[k], g_rsem.at[chip], row, 2 * k + core)

    def g_start(i, _):
        there = lax.rem(chip + i, 8)
        g_copy(there).start()
        return 0

    lax.fori_loop(1, 8, g_start, 0)

    def h_copy(k, mine):
        slot = 2 * k + mine
        return remote(g_all.at[slot], g_all.at[slot], h_ssem.at[k], h_rsem.at[k], row, mate)

    h_copy(chip, core).start()

    swap = remote(swap_out, swap_in, f_ssem, f_rsem, row, mate)
    swap.start()
    swap.wait_recv()
    hub[0, mate_pts, :] = swap_in[0:PTS, :]
    hub[0, 2 * PTS :, :] = (low + swap_in[PTS:, :].astype(F32)).astype(BF)

    def s_copy(n):
        return remote(hub.at[0], hub.at[n], s_ssem.at[n], s_rsem.at[n], 2 * around(z + HUBS[n]) + ylo, col)

    for n in (3, 4, 1, 2):
        s_copy(n).start()

    def a_copy(m, y):
        n, d = SECOND[m]
        plane = around(z - HUBS[n])
        return remote(
            hub.at[n], got.at[lax.rem(plane, 2), ylo, chip], a_ssem.at[m, y], a_rsem.at[lax.rem(plane, 2), ylo, chip],
            2 * around(z + d) + y, 2 * lax.div(plane, 2) + core,
        )

    def own_plane(n):
        return lax.div(around(z - HUBS[n]), 2) == chip

    def a_to_self(m, y):
        n, d = SECOND[m]
        return own_plane(n) & (ylo == y) if d == 0 else None

    def a_start(n):
        for m in range(len(SECOND)):
            if SECOND[m][0] == n:
                for y in range(2):
                    own = a_to_self(m, y)
                    if own is None:
                        a_copy(m, y).start()
                    else:
                        @pl.when(jnp.logical_not(own))
                        def _(m=m, y=y):
                            a_copy(m, y).start()

        @pl.when(own_plane(n))
        def _():
            got[lax.rem(around(z - HUBS[n]), 2), ylo, chip] = hub[n]

    a_start(0)

    w_copy = remote(w_ref, w_all.at[core], wb_ssem.at[0], wb_rsem.at[0], row, mate)
    b_copy = remote(b_ref, b_all.at[core], wb_ssem.at[1], wb_rsem.at[1], row, mate)
    w_copy.start()
    b_copy.start()

    for n in (1, 2, 3, 4):
        s_copy(n).wait_recv()
        a_start(n)

    loads[4].wait()
    loads[5].wait()
    w_copy.wait_recv()
    b_copy.wait_recv()

    def turn(i, _):
        e, t = lax.div(i, 4), lax.rem(i, 4)
        span = pl.ds(pl.multiple_of(t * 256, 256), 256)
        rows = pl.ds(pl.multiple_of(e * COLS + t * 256, 256), 256)
        w_turned[rows, :] = w_all[e, :, span].T
        b_turned[rows, :] = b_all[e, :, span].T
        return 0

    lax.fori_loop(0, 8, turn, 0)

    eye = onehot(iota((128, 128), 0) == iota((128, 128), 1))

    def arrive(e, y):
        def a_recv(i, _):
            @pl.when((hub_z[e] != z) | (ylo != y) | (i != chip))
            def _():
                remote(hub.at[0], got.at[e, y, i], a_ssem.at[0, 0], a_rsem.at[e, y, i], row, mate).wait_recv()

            return 0

        lax.fori_loop(0, 8, a_recv, 0)

    for e in range(2):
        for y in range(2):
            arrive(e, y)

    for e in range(2):
        for y in range(2):
            at = (2 * e + y) * ROWS
            rows = got[e, y, :, 0:64, :].reshape(ROWS, 128)
            turned[:, at : at + ROWS] = lax.dot_general(eye, rows, NT, preferred_element_type=F32)
            for g in range(4):
                low_f32[:, at + g * 128 : at + g * 128 + 128] = (
                    got[e, y, 2 * g, 64:80, :].astype(F32) + got[e, y, 2 * g + 1, 64:80, :].astype(F32)
                )

    left_e[...] = (turned[0:64, :] * turned[64:128, :]).astype(BF)

    def place(n, i, size):
        quarter = lax.rem(lax.div(z, 4) + QUARTERS[n][0] + 2 * lax.div(i, size), 4)
        return quarter * size + lax.rem(i, size)

    def build(n):
        bands_here = 3 * len(QUARTERS[n])

        def step(m, _):
            tile = turned[pl.ds(pl.multiple_of(m * 8, 8), 8), :]
            for p in range(SENT[n] // 16):
                pair = [
                    tile * low_f32[pl.ds(place(n, i, 3), 1), :] if i < bands_here else jnp.zeros_like(tile)
                    for i in (2 * p, 2 * p + 1)
                ]
                rows = pl.ds(pl.multiple_of(m * SENT[n] + 16 * p, 16), 16)
                left[rows, :] = jnp.concatenate(pair, axis=0).astype(BF)
            return 0

        lax.fori_loop(0, 8, step, 0)

    buffers = ((send0, recv0), (send1, recv1), (send2, recv2))

    def b_copy_to(n, m):
        sends, recvs = buffers[n]
        return remote(sends.at[m], recvs.at[chip], b_ssem.at[n, m], b_rsem.at[n, chip], row, 8 * core + m)

    for n in range(3):
        sends, recvs = buffers[n]
        build(n)

        def mul(t, _, n=n, sends=sends):
            span = pl.ds(pl.multiple_of(t * 256, 256), 256)
            size = SENT[n]
            d = jnp.dot(left[0 : 8 * size, :], w_turned[:, span], preferred_element_type=F32)
            if n == 0:
                e = jnp.dot(left_e[...], b_turned[:, span], preferred_element_type=F32)
                for m in range(8):
                    both = jnp.concatenate([d[m * size : m * size + 24], e[m * 8 : m * 8 + 8]], axis=0)
                    sends[m, :, span] = both.astype(BF)
            else:
                d = d.astype(BF)
                for m in range(8):
                    sends[m, :, span] = d[m * size : (m + 1) * size, :]
            return 0

        lax.fori_loop(0, 2, mul, 0)

        def b_start(m, _, n=n, sends=sends, recvs=recvs):
            @pl.when(8 * core + m != col)
            def _():
                b_copy_to(n, m).start()

            @pl.when(8 * core + m == col)
            def _():
                recvs[pl.ds(chip, 1)] = sends[pl.ds(m, 1)]

            return 0

        lax.fori_loop(0, 8, b_start, 0)

    def h_start(i, _):
        k = lax.rem(chip + i, 8)
        remote(g_all.at[col], g_all.at[2 * k + core], g_ssem.at[k], g_rsem.at[k], row, mate).wait_recv()
        h_copy(k, core).start()
        return 0

    lax.fori_loop(1, 8, h_start, 0)

    def h_wait(i, _):
        h_copy(i, 1 - core).wait_recv()
        return 0

    lax.fori_loop(0, 8, h_wait, 0)
    points = g_all[...].reshape(ROWS, NBP)
    mine = jnp.where(iota((8, 128), 1) == col * 8 + iota((8, 128), 0), pv_ref[...].astype(F32), 0.0)
    sel = onehot(jnp.sum(mine, axis=1, keepdims=True) == iota((8, NBP), 1).astype(F32))
    vpt = lax.dot_general(sel, points, NT, preferred_element_type=F32)
    sel = onehot((iota((16, NBP), 1) == iota((16, NBP), 0) + NB) & (iota((16, NBP), 0) < NCW))
    low_f32[:, 0:ROWS] = lax.dot_general(sel, points, NT, preferred_element_type=F32)

    def b_recv(n):
        recvs = buffers[n][1]

        def step(k, _):
            @pl.when(2 * k + lax.div(col, 8) != col)
            def _():
                remote(recvs.at[k], recvs.at[k], b_ssem.at[n, 0], b_rsem.at[n, k], row, mate).wait_recv()

            return 0

        lax.fori_loop(0, 8, step, 0)

    def c_copy(i):
        return remote(seg_out.at[i], seg_in.at[z], c_ssem.at[i], c_rsem.at[z], 2 * i + ylo, col)

    lane = iota((8, SEGP), 1)
    for n in range(3):
        recvs = buffers[n][1]
        count = 3 * len(QUARTERS[n])
        b_recv(n)
        d = recvs[0].astype(F32)
        for k in range(1, 8):
            d = d + recvs[k].astype(F32)
        if n == 0:
            exch = 2.0 * d[24:32]
        comb = [
            low_f32[pl.ds(place(n, i, 3), 1), 0:ROWS] * exch - vpt * d[i * 8 : i * 8 + 8] for i in range(count)
        ]
        if count == 3:
            comb.append(jnp.zeros_like(exch))
        comb = jnp.concatenate(comb, axis=0)
        head = comb.astype(BF)
        rest = (comb - head.astype(F32)).astype(BF)
        panel[0 : SENT[n], :] = jnp.dot(head, points, preferred_element_type=F32) + jnp.dot(
            rest, points, preferred_element_type=F32
        )
        for zl in range(4 * len(QUARTERS[n])):
            halves = []
            for y in range(2):
                start = SEG * (2 * zl + y)
                band0, off = start // NB, start % NB
                seg = panel[band0 * 8 : band0 * 8 + 8, :]
                if off:
                    seg = pltpu.roll(seg, NBP - off, 1)
                seg = seg[:, 0:SEGP]
                if off + SEG > NB:
                    more = pltpu.roll(panel[band0 * 8 + 8 : band0 * 8 + 16, :], NB - off, 1)[:, 0:SEGP]
                    seg = jnp.where(lane < NB - off, seg, more)
                halves.append(seg)
            seg_out[pl.ds(place(n, jnp.int32(zl), 4), 1)] = jnp.concatenate(halves, axis=0).astype(BF).reshape(1, 16, SEGP)

        def c_start(i, _, n=n):
            there = place(n, i, 4)

            @pl.when(there != z)
            def _():
                c_copy(there).start()

            @pl.when(there == z)
            def _():
                seg_in[pl.ds(z, 1)] = seg_out[pl.ds(z, 1)]

            return 0

        lax.fori_loop(0, 4 * len(QUARTERS[n]), c_start, 0)

    def c_recv(i, _):
        @pl.when(i != z)
        def _():
            remote(seg_out.at[i], seg_in.at[i], c_ssem.at[i], c_rsem.at[i], row, mate).wait_recv()

        return 0

    lax.fori_loop(0, NZ, c_recv, 0)
    acc = seg_in[0].astype(F32)
    for i in range(1, NZ):
        acc = acc + seg_in[i].astype(F32)
    total[...] = acc.reshape(2, 8, SEGP)
    y_copy = remote(total.at[1 - ylo], y_in, y_ssem, y_rsem, other_row, col)
    y_copy.start()

    def drain(i, _):
        @pl.when(i != z)
        def _():
            c_copy(i).wait_send()

        return 0

    lax.fori_loop(0, NZ, drain, 0)
    for n in range(1, 5):
        s_copy(n).wait_send()
    for m in range(len(SECOND)):
        for y in range(2):
            own = a_to_self(m, y)
            if own is None:
                a_copy(m, y).wait_send()
            else:
                @pl.when(jnp.logical_not(own))
                def _(m=m, y=y):
                    a_copy(m, y).wait_send()

    def drain8(i, _):
        @pl.when(i != chip)
        def _():
            g_copy(i).wait_send()

        h_copy(i, core).wait_send()

        @pl.when(8 * core + i != col)
        def _():
            for n in range(3):
                b_copy_to(n, i).wait_send()

        return 0

    lax.fori_loop(0, 8, drain8, 0)
    swap.wait_send()
    w_copy.wait_send()
    b_copy.wait_send()
    y_copy.wait()
    out_ref[...] = total[ylo] + y_in[...]


def body(orb_valence, orb_conduction, screened, bare, panel_valence, panel_conduction):
    vmem = pl.BlockSpec(memory_space=pltpu.VMEM)
    hbm = pl.BlockSpec(memory_space=pl.ANY)
    dma = pltpu.SemaphoreType.DMA
    out = pl.pallas_call(
        kernel,
        out_shape=jax.ShapeDtypeStruct((8, SEGP), F32),
        in_specs=[hbm] * 6,
        out_specs=vmem,
        scratch_shapes=[
            pltpu.VMEM((PTS, NB), BF),
            pltpu.VMEM((PTS, NB), BF),
            pltpu.VMEM((1, 128), jnp.int32),
            pltpu.VMEM((1, 128), jnp.int32),
            pltpu.VMEM((5, 80, 128), BF),
            pltpu.VMEM((128, NB), BF),
            pltpu.VMEM((NCOL, PTS, NBP), BF),
            pltpu.VMEM((48, 128), BF),
            pltpu.VMEM((48, 128), BF),
            pltpu.VMEM((2, 2, 8, 80, 128), BF),
            pltpu.VMEM((16, 2 * COLS), F32),
            pltpu.VMEM((128, 2 * COLS), F32),
            pltpu.VMEM((8 * 48, 2 * COLS), BF),
            pltpu.VMEM((64, 2 * COLS), BF),
            pltpu.VMEM((2, ROWS, COLS), BF),
            pltpu.VMEM((2, ROWS, COLS), BF),
            pltpu.VMEM((2 * COLS, ROWS), BF),
            pltpu.VMEM((2 * COLS, ROWS), BF),
            pltpu.VMEM((8, 32, ROWS), BF),
            pltpu.VMEM((8, 48, ROWS), BF),
            pltpu.VMEM((8, 32, ROWS), BF),
            pltpu.VMEM((8, 32, ROWS), BF),
            pltpu.VMEM((8, 48, ROWS), BF),
            pltpu.VMEM((8, 32, ROWS), BF),
            pltpu.VMEM((48, NBP), F32),
            pltpu.VMEM((NZ, 16, SEGP), BF),
            pltpu.VMEM((NZ, 16, SEGP), BF),
            pltpu.VMEM((2, 8, SEGP), F32),
            pltpu.VMEM((8, SEGP), F32),
            dma((6,)),
            dma((2,)), dma((2,)),
            dma((len(SECOND), 2)), dma((2, 2, 8)),
            dma((5,)), dma((5,)),
            dma((8,)), dma((8,)),
            dma((8,)), dma((8,)),
            dma, dma,
            dma((3, 8)), dma((3, 8)),
            dma((16,)), dma((16,)),
            dma, dma,
        ],
        compiler_params=pltpu.CompilerParams(
            collective_id=0, has_side_effects=True, vmem_limit_bytes=60 * 2**20
        ),
        name="kernel_panel",
    )(
        orb_valence, orb_conduction, panel_valence.reshape(1, -1), panel_conduction.reshape(1, -1),
        screened, bare,
    )
    return out[:, :SEG].T


def solution(mesh):
    placed = (
        P(("prow", "pcol"), None),
        P(("prow", "pcol"), None),
        P("prow", "pcol"),
        P("prow", "pcol"),
        P(),
        P(),
    )
    return jax.shard_map(
        body, mesh=mesh, in_specs=placed, out_specs=P("prow", "pcol"), check_vma=False
    )
```

```python
import jax
import jax.numpy as jnp
from jax import lax
from jax.experimental import pallas as pl
from jax.experimental.pallas import tpu as pltpu
from jax.sharding import PartitionSpec as P

NCW = 12
NZ = 16
NCOL = 16
PTS = 32
ROWS = PTS * NCOL
COLS = 1024
NB = 1000
NBP = 1024
QUARTERS = ((2,), (1, 3), (0,))
SENT = (32, 48, 32)
SEG = 375
SEGP = 384
HUBS = (0, 3, -3, 6, -6)
SECOND = tuple((n, d) for n in range(5) for d in ((-1, 0, 1, 2) if n == 3 else (-1, 0, 1)))
BF = jnp.bfloat16
F32 = jnp.float32
MESH = pl.DeviceIdType.MESH
NT = (((1,), (1,)), ((), ()))


def iota(shape, dim):
    return lax.broadcasted_iota(jnp.int32, shape, dim)


def onehot(mask):
    return jnp.where(mask, 1.0, 0.0).astype(BF)


def kernel(
    v_hbm, c_hbm, pv_hbm, pc_hbm, w_ref, b_ref, out_ref,
    v_ref, c_ref, pv_ref, pc_ref,
    hub, cpad, g_all, swap_out, swap_in, got, low_f32, turned, left, left_e,
    w_all, b_all, w_turned, b_turned, send0, send1, send2, recv0, recv1, recv2, panel, seg_out, seg_in, total, y_in,
    loc_sem, wb_ssem, wb_rsem, a_ssem, a_rsem, s_ssem, s_rsem, g_ssem, g_rsem, h_ssem, h_rsem,
    f_ssem, f_rsem, b_ssem, b_rsem, c_ssem, c_rsem, y_ssem, y_rsem,
):
    row = lax.axis_index("prow")
    col = lax.axis_index("pcol")
    z = lax.div(row, 2)
    ylo = lax.rem(row, 2)
    core = lax.rem(col, 2)
    chip = lax.div(col, 2)
    mate = col + 1 - 2 * core
    other_row = row + 1 - 2 * ylo

    def around(i):
        return lax.rem(i + NZ, NZ)

    def remote(src, dst, ssem, rsem, prow, pcol):
        return pltpu.make_async_remote_copy(
            src_ref=src, dst_ref=dst, send_sem=ssem, recv_sem=rsem,
            device_id={"prow": prow, "pcol": pcol}, device_id_type=MESH,
        )

    loads = [
        pltpu.make_async_copy(src, dst, loc_sem.at[n])
        for n, (src, dst) in enumerate(
            ((c_hbm, c_ref), (pc_hbm, pc_ref), (v_hbm, v_ref), (pv_hbm, pv_ref), (w_ref, w_all.at[core]), (b_ref, b_all.at[core]))
        )
    ]
    for copy in loads:
        copy.start()

    barrier = pltpu.get_barrier_semaphore()

    def greet(prow, pcol):
        pl.semaphore_signal(barrier, inc=1, device_id={"prow": prow, "pcol": pcol}, device_id_type=MESH)

    def step_of(plane):
        ahead = around(z - plane)
        back = 1 - lax.rem(17 - ahead, 3)
        return jnp.where(ahead > 8, back, jnp.where(ahead == 8, 2, lax.rem(ahead + 1, 3) - 1))

    hub_z = [around(z - step_of(2 * chip + e)) for e in range(2)]

    for n in (4, 3, 2, 1):
        greet(2 * around(z - HUBS[n]) + ylo, col)
    greet(other_row, col)

    def greet_step(i, _):
        for e in range(2):
            for y in range(2):
                @pl.when((hub_z[e] != z) | (ylo != y) | (i != chip))
                def _(e=e, y=y):
                    greet(2 * hub_z[e] + y, 2 * i + core)

        return 0

    lax.fori_loop(0, 8, greet_step, 0)

    def greet_line(i, _):
        @pl.when(i != col)
        def _():
            greet(row, i)

        return 0

    lax.fori_loop(0, NZ, greet_line, 0)

    for copy in loads[:4]:
        copy.wait()
    val = v_ref[...]
    con = c_ref[...]
    bands = iota((NB, 128), 0)
    lanes = iota((NB, 128), 1)
    vp = jnp.dot(val, onehot(bands == pv_ref[...]), preferred_element_type=F32)
    cp = jnp.dot(con, onehot(bands == pc_ref[...]), preferred_element_type=F32)
    lane = iota((PTS, 128), 1)
    first = jnp.where(lane < 64, cp, pltpu.roll(vp, 64, 1))
    second = jnp.where(lane < 64, pltpu.roll(cp, 64, 1), vp)
    cpad[...] = jnp.zeros((128, NB), BF)
    cpad[pl.ds(pl.multiple_of(lax.rem(col, 4) * PTS, PTS), PTS), :] = con
    low_rows = iota((16, NB), 0)
    low_sel = onehot((low_rows == iota((16, NB), 1)) & (low_rows < NCW))
    low = lax.dot_general(low_sel, cpad[...], NT, preferred_element_type=F32)
    swap_out[0:PTS, :] = jnp.where(core == 0, second, first).astype(BF)
    swap_out[PTS:, :] = low.astype(BF)
    own_pts = pl.ds(pl.multiple_of(core * PTS, PTS), PTS)
    mate_pts = pl.ds(pl.multiple_of((1 - core) * PTS, PTS), PTS)
    hub[0, own_pts, :] = jnp.where(core == 0, first, second).astype(BF)
    tail = jnp.dot(val, onehot((bands == lanes + 896) & (lanes < 104)), preferred_element_type=F32)
    tail = tail + jnp.dot(con, onehot((bands + 104 == lanes) & (bands < NCW)), preferred_element_type=F32)
    g_all[pl.ds(col, 1), :, 0:896] = val[:, 0:896].reshape(1, PTS, 896)
    g_all[pl.ds(col, 1), :, 896:NBP] = tail.astype(BF).reshape(1, PTS, 128)

    pl.semaphore_wait(barrier, 52 - jnp.where((hub_z[0] == z) | (hub_z[1] == z), 1, 0))
    def g_copy(k):
        return remote(g_all.at[col], g_all.at[col], g_ssem.at[k], g_rsem.at[chip], row, 2 * k + core)

    def g_start(i, _):
        there = lax.rem(chip + i, 8)
        g_copy(there).start()
        return 0

    lax.fori_loop(1, 8, g_start, 0)

    def h_copy(k, mine):
        slot = 2 * k + mine
        return remote(g_all.at[slot], g_all.at[slot], h_ssem.at[k], h_rsem.at[k], row, mate)

    h_copy(chip, core).start()

    swap = remote(swap_out, swap_in, f_ssem, f_rsem, row, mate)
    swap.start()
    swap.wait_recv()
    hub[0, mate_pts, :] = swap_in[0:PTS, :]
    hub[0, 2 * PTS :, :] = (low + swap_in[PTS:, :].astype(F32)).astype(BF)

    def s_copy(n):
        return remote(hub.at[0], hub.at[n], s_ssem.at[n], s_rsem.at[n], 2 * around(z + HUBS[n]) + ylo, col)

    for n in (3, 4, 1, 2):
        s_copy(n).start()

    def a_copy(m, y):
        n, d = SECOND[m]
        plane = around(z - HUBS[n])
        return remote(
            hub.at[n], got.at[lax.rem(plane, 2), ylo, chip], a_ssem.at[m, y], a_rsem.at[lax.rem(plane, 2), ylo, chip],
            2 * around(z + d) + y, 2 * lax.div(plane, 2) + core,
        )

    def own_plane(n):
        return lax.div(around(z - HUBS[n]), 2) == chip

    def a_to_self(m, y):
        n, d = SECOND[m]
        return own_plane(n) & (ylo == y) if d == 0 else None

    def a_start(n):
        for m in range(len(SECOND)):
            if SECOND[m][0] == n:
                for y in range(2):
                    own = a_to_self(m, y)
                    if own is None:
                        a_copy(m, y).start()
                    else:
                        @pl.when(jnp.logical_not(own))
                        def _(m=m, y=y):
                            a_copy(m, y).start()

        @pl.when(own_plane(n))
        def _():
            got[lax.rem(around(z - HUBS[n]), 2), ylo, chip] = hub[n]

    a_start(0)

    w_copy = remote(w_ref, w_all.at[core], wb_ssem.at[0], wb_rsem.at[0], row, mate)
    b_copy = remote(b_ref, b_all.at[core], wb_ssem.at[1], wb_rsem.at[1], row, mate)
    w_copy.start()
    b_copy.start()

    for n in (1, 2, 3, 4):
        s_copy(n).wait_recv()
        a_start(n)

    def h_start(i, _):
        k = lax.rem(chip + i, 8)
        remote(g_all.at[col], g_all.at[2 * k + core], g_ssem.at[k], g_rsem.at[k], row, mate).wait_recv()
        h_copy(k, core).start()
        return 0

    lax.fori_loop(1, 8, h_start, 0)

    loads[4].wait()
    loads[5].wait()
    w_copy.wait_recv()
    b_copy.wait_recv()

    def turn(i, _):
        e, t = lax.div(i, 4), lax.rem(i, 4)
        span = pl.ds(pl.multiple_of(t * 256, 256), 256)
        rows = pl.ds(pl.multiple_of(e * COLS + t * 256, 256), 256)
        w_turned[rows, :] = w_all[e, :, span].T
        b_turned[rows, :] = b_all[e, :, span].T
        return 0

    lax.fori_loop(0, 8, turn, 0)

    eye = onehot(iota((128, 128), 0) == iota((128, 128), 1))

    def arrive(e, y):
        def a_recv(i, _):
            @pl.when((hub_z[e] != z) | (ylo != y) | (i != chip))
            def _():
                remote(hub.at[0], got.at[e, y, i], a_ssem.at[0, 0], a_rsem.at[e, y, i], row, mate).wait_recv()

            return 0

        lax.fori_loop(0, 8, a_recv, 0)

    for e in range(2):
        for y in range(2):
            arrive(e, y)

    for e in range(2):
        for y in range(2):
            at = (2 * e + y) * ROWS
            rows = got[e, y, :, 0:64, :].reshape(ROWS, 128)
            turned[:, at : at + ROWS] = lax.dot_general(eye, rows, NT, preferred_element_type=F32)
            for g in range(4):
                low_f32[:, at + g * 128 : at + g * 128 + 128] = (
                    got[e, y, 2 * g, 64:80, :].astype(F32) + got[e, y, 2 * g + 1, 64:80, :].astype(F32)
                )

    left_e[...] = (turned[0:64, :] * turned[64:128, :]).astype(BF)

    def place(n, i, size):
        quarter = lax.rem(lax.div(z, 4) + QUARTERS[n][0] + 2 * lax.div(i, size), 4)
        return quarter * size + lax.rem(i, size)

    def build(n):
        bands_here = 3 * len(QUARTERS[n])

        def step(m, _):
            tile = turned[pl.ds(pl.multiple_of(m * 8, 8), 8), :]
            for p in range(SENT[n] // 16):
                pair = [
                    tile * low_f32[pl.ds(place(n, i, 3), 1), :] if i < bands_here else jnp.zeros_like(tile)
                    for i in (2 * p, 2 * p + 1)
                ]
                rows = pl.ds(pl.multiple_of(m * SENT[n] + 16 * p, 16), 16)
                left[rows, :] = jnp.concatenate(pair, axis=0).astype(BF)
            return 0

        lax.fori_loop(0, 8, step, 0)

    buffers = ((send0, recv0), (send1, recv1), (send2, recv2))

    def b_copy_to(n, m):
        sends, recvs = buffers[n]
        return remote(sends.at[m], recvs.at[chip], b_ssem.at[n, m], b_rsem.at[n, chip], row, 8 * core + m)

    for n in range(3):
        sends, recvs = buffers[n]
        build(n)

        def mul(t, _, n=n, sends=sends):
            span = pl.ds(pl.multiple_of(t * 256, 256), 256)
            size = SENT[n]
            d = jnp.dot(left[0 : 8 * size, :], w_turned[:, span], preferred_element_type=F32)
            if n == 0:
                e = jnp.dot(left_e[...], b_turned[:, span], preferred_element_type=F32)
                for m in range(8):
                    both = jnp.concatenate([d[m * size : m * size + 24], e[m * 8 : m * 8 + 8]], axis=0)
                    sends[m, :, span] = both.astype(BF)
            else:
                d = d.astype(BF)
                for m in range(8):
                    sends[m, :, span] = d[m * size : (m + 1) * size, :]
            return 0

        lax.fori_loop(0, 2, mul, 0)

        def b_start(m, _, n=n, sends=sends, recvs=recvs):
            @pl.when(8 * core + m != col)
            def _():
                b_copy_to(n, m).start()

            @pl.when(8 * core + m == col)
            def _():
                recvs[pl.ds(chip, 1)] = sends[pl.ds(m, 1)]

            return 0

        lax.fori_loop(0, 8, b_start, 0)

    def h_wait(i, _):
        h_copy(i, 1 - core).wait_recv()
        return 0

    lax.fori_loop(0, 8, h_wait, 0)
    points = g_all[...].reshape(ROWS, NBP)
    mine = jnp.where(iota((8, 128), 1) == col * 8 + iota((8, 128), 0), pv_ref[...].astype(F32), 0.0)
    sel = onehot(jnp.sum(mine, axis=1, keepdims=True) == iota((8, NBP), 1).astype(F32))
    vpt = lax.dot_general(sel, points, NT, preferred_element_type=F32)
    sel = onehot((iota((16, NBP), 1) == iota((16, NBP), 0) + NB) & (iota((16, NBP), 0) < NCW))
    low_f32[:, 0:ROWS] = lax.dot_general(sel, points, NT, preferred_element_type=F32)

    def b_recv(n):
        recvs = buffers[n][1]

        def step(k, _):
            @pl.when(2 * k + lax.div(col, 8) != col)
            def _():
                remote(recvs.at[k], recvs.at[k], b_ssem.at[n, 0], b_rsem.at[n, k], row, mate).wait_recv()

            return 0

        lax.fori_loop(0, 8, step, 0)

    def c_copy(i):
        return remote(seg_out.at[i], seg_in.at[z], c_ssem.at[i], c_rsem.at[z], 2 * i + ylo, col)

    lane = iota((8, SEGP), 1)
    for n in range(3):
        recvs = buffers[n][1]
        count = 3 * len(QUARTERS[n])
        b_recv(n)
        d = recvs[0].astype(F32)
        for k in range(1, 8):
            d = d + recvs[k].astype(F32)
        if n == 0:
            exch = 2.0 * d[24:32]
        comb = [
            low_f32[pl.ds(place(n, i, 3), 1), 0:ROWS] * exch - vpt * d[i * 8 : i * 8 + 8] for i in range(count)
        ]
        if count == 3:
            comb.append(jnp.zeros_like(exch))
        comb = jnp.concatenate(comb, axis=0)
        head = comb.astype(BF)
        rest = (comb - head.astype(F32)).astype(BF)
        panel[0 : SENT[n], :] = jnp.dot(head, points, preferred_element_type=F32) + jnp.dot(
            rest, points, preferred_element_type=F32
        )
        for zl in range(4 * len(QUARTERS[n])):
            halves = []
            for y in range(2):
                start = SEG * (2 * zl + y)
                band0, off = start // NB, start % NB
                seg = panel[band0 * 8 : band0 * 8 + 8, :]
                if off:
                    seg = pltpu.roll(seg, NBP - off, 1)
                seg = seg[:, 0:SEGP]
                if off + SEG > NB:
                    more = pltpu.roll(panel[band0 * 8 + 8 : band0 * 8 + 16, :], NB - off, 1)[:, 0:SEGP]
                    seg = jnp.where(lane < NB - off, seg, more)
                halves.append(seg)
            seg_out[pl.ds(place(n, jnp.int32(zl), 4), 1)] = jnp.concatenate(halves, axis=0).astype(BF).reshape(1, 16, SEGP)

        def c_start(i, _, n=n):
            there = place(n, i, 4)

            @pl.when(there != z)
            def _():
                c_copy(there).start()

            @pl.when(there == z)
            def _():
                seg_in[pl.ds(z, 1)] = seg_out[pl.ds(z, 1)]

            return 0

        lax.fori_loop(0, 4 * len(QUARTERS[n]), c_start, 0)

    def c_recv(i, _):
        @pl.when(i != z)
        def _():
            remote(seg_out.at[i], seg_in.at[i], c_ssem.at[i], c_rsem.at[i], row, mate).wait_recv()

        return 0

    lax.fori_loop(0, NZ, c_recv, 0)
    acc = seg_in[0].astype(F32)
    for i in range(1, NZ):
        acc = acc + seg_in[i].astype(F32)
    total[...] = acc.reshape(2, 8, SEGP)
    y_copy = remote(total.at[1 - ylo], y_in, y_ssem, y_rsem, other_row, col)
    y_copy.start()

    def drain(i, _):
        @pl.when(i != z)
        def _():
            c_copy(i).wait_send()

        return 0

    lax.fori_loop(0, NZ, drain, 0)
    for n in range(1, 5):
        s_copy(n).wait_send()
    for m in range(len(SECOND)):
        for y in range(2):
            own = a_to_self(m, y)
            if own is None:
                a_copy(m, y).wait_send()
            else:
                @pl.when(jnp.logical_not(own))
                def _(m=m, y=y):
                    a_copy(m, y).wait_send()

    def drain8(i, _):
        @pl.when(i != chip)
        def _():
            g_copy(i).wait_send()

        h_copy(i, core).wait_send()

        @pl.when(8 * core + i != col)
        def _():
            for n in range(3):
                b_copy_to(n, i).wait_send()

        return 0

    lax.fori_loop(0, 8, drain8, 0)
    swap.wait_send()
    w_copy.wait_send()
    b_copy.wait_send()
    y_copy.wait()
    out_ref[...] = total[ylo] + y_in[...]


def body(orb_valence, orb_conduction, screened, bare, panel_valence, panel_conduction):
    vmem = pl.BlockSpec(memory_space=pltpu.VMEM)
    hbm = pl.BlockSpec(memory_space=pl.ANY)
    dma = pltpu.SemaphoreType.DMA
    out = pl.pallas_call(
        kernel,
        out_shape=jax.ShapeDtypeStruct((8, SEGP), F32),
        in_specs=[hbm] * 6,
        out_specs=vmem,
        scratch_shapes=[
            pltpu.VMEM((PTS, NB), BF),
            pltpu.VMEM((PTS, NB), BF),
            pltpu.VMEM((1, 128), jnp.int32),
            pltpu.VMEM((1, 128), jnp.int32),
            pltpu.VMEM((5, 80, 128), BF),
            pltpu.VMEM((128, NB), BF),
            pltpu.VMEM((NCOL, PTS, NBP), BF),
            pltpu.VMEM((48, 128), BF),
            pltpu.VMEM((48, 128), BF),
            pltpu.VMEM((2, 2, 8, 80, 128), BF),
            pltpu.VMEM((16, 2 * COLS), F32),
            pltpu.VMEM((128, 2 * COLS), F32),
            pltpu.VMEM((8 * 48, 2 * COLS), BF),
            pltpu.VMEM((64, 2 * COLS), BF),
            pltpu.VMEM((2, ROWS, COLS), BF),
            pltpu.VMEM((2, ROWS, COLS), BF),
            pltpu.VMEM((2 * COLS, ROWS), BF),
            pltpu.VMEM((2 * COLS, ROWS), BF),
            pltpu.VMEM((8, 32, ROWS), BF),
            pltpu.VMEM((8, 48, ROWS), BF),
            pltpu.VMEM((8, 32, ROWS), BF),
            pltpu.VMEM((8, 32, ROWS), BF),
            pltpu.VMEM((8, 48, ROWS), BF),
            pltpu.VMEM((8, 32, ROWS), BF),
            pltpu.VMEM((48, NBP), F32),
            pltpu.VMEM((NZ, 16, SEGP), BF),
            pltpu.VMEM((NZ, 16, SEGP), BF),
            pltpu.VMEM((2, 8, SEGP), F32),
            pltpu.VMEM((8, SEGP), F32),
            dma((6,)),
            dma((2,)), dma((2,)),
            dma((len(SECOND), 2)), dma((2, 2, 8)),
            dma((5,)), dma((5,)),
            dma((8,)), dma((8,)),
            dma((8,)), dma((8,)),
            dma, dma,
            dma((3, 8)), dma((3, 8)),
            dma((16,)), dma((16,)),
            dma, dma,
        ],
        compiler_params=pltpu.CompilerParams(
            collective_id=0, has_side_effects=True, vmem_limit_bytes=60 * 2**20
        ),
        name="kernel_panel",
    )(
        orb_valence, orb_conduction, panel_valence.reshape(1, -1), panel_conduction.reshape(1, -1),
        screened, bare,
    )
    return out[:, :SEG].T


def solution(mesh):
    placed = (
        P(("prow", "pcol"), None),
        P(("prow", "pcol"), None),
        P("prow", "pcol"),
        P("prow", "pcol"),
        P(),
        P(),
    )
    return jax.shard_map(
        body, mesh=mesh, in_specs=placed, out_specs=P("prow", "pcol"), check_vma=False
    )
```

```python
import jax
import jax.numpy as jnp
from jax import lax
from jax.experimental import pallas as pl
from jax.experimental.pallas import tpu as pltpu
from jax.sharding import PartitionSpec as P

NCW = 12
NZ = 16
NCOL = 16
PTS = 32
ROWS = PTS * NCOL
COLS = 1024
NB = 1000
NBP = 1024
QUARTERS = ((2,), (1, 3), (0,))
SENT = (32, 48, 32)
SEG = 375
SEGP = 384
HUBS = (0, 3, -3, 6, -6)
SECOND = tuple((n, d) for n in range(5) for d in ((-1, 0, 1, 2) if n == 3 else (-1, 0, 1)))
BF = jnp.bfloat16
F32 = jnp.float32
MESH = pl.DeviceIdType.MESH
NT = (((1,), (1,)), ((), ()))


def iota(shape, dim):
    return lax.broadcasted_iota(jnp.int32, shape, dim)


def onehot(mask):
    return jnp.where(mask, 1.0, 0.0).astype(BF)


def kernel(
    v_hbm, c_hbm, pv_hbm, pc_hbm, w_ref, b_ref, out_ref,
    v_ref, c_ref, pv_ref, pc_ref,
    hub, cpad, g_all, row_low, row_vp, swap_out, swap_in, got, low_f32, turned, left, left_e,
    w_all, b_all, w_turned, b_turned, send0, send1, send2, recv0, recv1, recv2, panel, seg_out, seg_in, total, y_in,
    loc_sem, wb_ssem, wb_rsem, a_ssem, a_rsem, s_ssem, s_rsem, g_ssem, g_rsem, h_ssem, h_rsem,
    f_ssem, f_rsem, b_ssem, b_rsem, c_ssem, c_rsem, y_ssem, y_rsem,
):
    row = lax.axis_index("prow")
    col = lax.axis_index("pcol")
    z = lax.div(row, 2)
    ylo = lax.rem(row, 2)
    core = lax.rem(col, 2)
    chip = lax.div(col, 2)
    mate = col + 1 - 2 * core
    other_row = row + 1 - 2 * ylo

    def around(i):
        return lax.rem(i + NZ, NZ)

    def remote(src, dst, ssem, rsem, prow, pcol):
        return pltpu.make_async_remote_copy(
            src_ref=src, dst_ref=dst, send_sem=ssem, recv_sem=rsem,
            device_id={"prow": prow, "pcol": pcol}, device_id_type=MESH,
        )

    loads = [
        pltpu.make_async_copy(src, dst, loc_sem.at[n])
        for n, (src, dst) in enumerate(
            ((c_hbm, c_ref), (pc_hbm, pc_ref), (v_hbm, v_ref), (pv_hbm, pv_ref), (w_ref, w_all.at[core]), (b_ref, b_all.at[core]))
        )
    ]
    for copy in loads:
        copy.start()

    barrier = pltpu.get_barrier_semaphore()

    def greet(prow, pcol):
        pl.semaphore_signal(barrier, inc=1, device_id={"prow": prow, "pcol": pcol}, device_id_type=MESH)

    def step_of(plane):
        ahead = around(z - plane)
        back = 1 - lax.rem(17 - ahead, 3)
        return jnp.where(ahead > 8, back, jnp.where(ahead == 8, 2, lax.rem(ahead + 1, 3) - 1))

    hub_z = [around(z - step_of(2 * chip + e)) for e in range(2)]

    for n in (4, 3, 2, 1):
        greet(2 * around(z - HUBS[n]) + ylo, col)
    greet(other_row, col)

    def greet_step(i, _):
        for e in range(2):
            for y in range(2):
                @pl.when((hub_z[e] != z) | (ylo != y) | (i != chip))
                def _(e=e, y=y):
                    greet(2 * hub_z[e] + y, 2 * i + core)

        return 0

    lax.fori_loop(0, 8, greet_step, 0)

    def greet_line(i, _):
        @pl.when(i != col)
        def _():
            greet(row, i)

        return 0

    lax.fori_loop(0, NZ, greet_line, 0)

    for copy in loads[:4]:
        copy.wait()
    val = v_ref[...]
    con = c_ref[...]
    bands = iota((NB, 128), 0)
    lanes = iota((NB, 128), 1)
    vp = jnp.dot(val, onehot(bands == pv_ref[...]), preferred_element_type=F32)
    cp = jnp.dot(con, onehot(bands == pc_ref[...]), preferred_element_type=F32)
    lane = iota((PTS, 128), 1)
    first = jnp.where(lane < 64, cp, pltpu.roll(vp, 64, 1))
    second = jnp.where(lane < 64, pltpu.roll(cp, 64, 1), vp)
    cpad[...] = jnp.zeros((128, NB), BF)
    cpad[pl.ds(pl.multiple_of(lax.rem(col, 4) * PTS, PTS), PTS), :] = con
    low_rows = iota((16, NB), 0)
    low_sel = onehot((low_rows == iota((16, NB), 1)) & (low_rows < NCW))
    low = lax.dot_general(low_sel, cpad[...], NT, preferred_element_type=F32)
    swap_out[0:PTS, :] = jnp.where(core == 0, second, first).astype(BF)
    swap_out[PTS:, :] = low.astype(BF)
    own_pts = pl.ds(pl.multiple_of(core * PTS, PTS), PTS)
    mate_pts = pl.ds(pl.multiple_of((1 - core) * PTS, PTS), PTS)
    hub[0, own_pts, :] = jnp.where(core == 0, first, second).astype(BF)
    tail = jnp.dot(val, onehot((bands == lanes + 896) & (lanes < 104)), preferred_element_type=F32)
    tail = tail + jnp.dot(con, onehot((bands + 104 == lanes) & (bands < NCW)), preferred_element_type=F32)
    g_all[pl.ds(col, 1), :, 0:896] = val[:, 0:896].reshape(1, PTS, 896)
    g_all[pl.ds(col, 1), :, 896:NBP] = tail.astype(BF).reshape(1, PTS, 128)

    pl.semaphore_wait(barrier, 52 - jnp.where((hub_z[0] == z) | (hub_z[1] == z), 1, 0))
    def g_copy(k):
        return remote(g_all.at[col], g_all.at[col], g_ssem.at[k], g_rsem.at[chip], row, 2 * k + core)

    def g_start(i, _):
        there = lax.rem(chip + i, 8)
        g_copy(there).start()
        return 0

    lax.fori_loop(1, 8, g_start, 0)

    def h_copy(k, mine):
        slot = 2 * k + mine
        return remote(g_all.at[slot], g_all.at[slot], h_ssem.at[k], h_rsem.at[k], row, mate)

    h_copy(chip, core).start()

    swap = remote(swap_out, swap_in, f_ssem, f_rsem, row, mate)
    swap.start()
    swap.wait_recv()
    hub[0, mate_pts, :] = swap_in[0:PTS, :]
    hub[0, 2 * PTS :, :] = (low + swap_in[PTS:, :].astype(F32)).astype(BF)

    def s_copy(n):
        return remote(hub.at[0], hub.at[n], s_ssem.at[n], s_rsem.at[n], 2 * around(z + HUBS[n]) + ylo, col)

    for n in (3, 4, 1, 2):
        s_copy(n).start()

    def a_copy(m, y):
        n, d = SECOND[m]
        plane = around(z - HUBS[n])
        return remote(
            hub.at[n], got.at[lax.rem(plane, 2), ylo, chip], a_ssem.at[m, y], a_rsem.at[lax.rem(plane, 2), ylo, chip],
            2 * around(z + d) + y, 2 * lax.div(plane, 2) + core,
        )

    def own_plane(n):
        return lax.div(around(z - HUBS[n]), 2) == chip

    def a_to_self(m, y):
        n, d = SECOND[m]
        return own_plane(n) & (ylo == y) if d == 0 else None

    def a_start(n):
        for m in range(len(SECOND)):
            if SECOND[m][0] == n:
                for y in range(2):
                    own = a_to_self(m, y)
                    if own is None:
                        a_copy(m, y).start()
                    else:
                        @pl.when(jnp.logical_not(own))
                        def _(m=m, y=y):
                            a_copy(m, y).start()

        @pl.when(own_plane(n))
        def _():
            got[lax.rem(around(z - HUBS[n]), 2), ylo, chip] = hub[n]

    a_start(0)

    w_copy = remote(w_ref, w_all.at[core], wb_ssem.at[0], wb_rsem.at[0], row, mate)
    b_copy = remote(b_ref, b_all.at[core], wb_ssem.at[1], wb_rsem.at[1], row, mate)
    w_copy.start()
    b_copy.start()

    for n in (1, 2, 3, 4):
        s_copy(n).wait_recv()
        a_start(n)

    def h_start(i, _):
        k = lax.rem(chip + i, 8)
        remote(g_all.at[col], g_all.at[2 * k + core], g_ssem.at[k], g_rsem.at[k], row, mate).wait_recv()
        h_copy(k, core).start()
        return 0

    lax.fori_loop(1, 8, h_start, 0)

    loads[4].wait()
    loads[5].wait()
    w_copy.wait_recv()
    b_copy.wait_recv()

    def turn(i, _):
        e, t = lax.div(i, 4), lax.rem(i, 4)
        span = pl.ds(pl.multiple_of(t * 256, 256), 256)
        rows = pl.ds(pl.multiple_of(e * COLS + t * 256, 256), 256)
        w_turned[rows, :] = w_all[e, :, span].T
        b_turned[rows, :] = b_all[e, :, span].T
        return 0

    lax.fori_loop(0, 8, turn, 0)

    def h_wait(i, _):
        h_copy(i, 1 - core).wait_recv()
        return 0

    lax.fori_loop(0, 8, h_wait, 0)
    mine = jnp.where(iota((8, 128), 1) == col * 8 + iota((8, 128), 0), pv_ref[...].astype(F32), 0.0)
    sel = onehot(jnp.sum(mine, axis=1, keepdims=True) == iota((8, NBP), 1).astype(F32))
    row_vp[...] = lax.dot_general(sel, g_all[...].reshape(ROWS, NBP), NT, preferred_element_type=F32)
    sel = onehot((iota((16, NBP), 1) == iota((16, NBP), 0) + NB) & (iota((16, NBP), 0) < NCW))
    row_low[...] = lax.dot_general(sel, g_all[...].reshape(ROWS, NBP), NT, preferred_element_type=F32)

    eye = onehot(iota((128, 128), 0) == iota((128, 128), 1))

    def arrive(e, y):
        def a_recv(i, _):
            @pl.when((hub_z[e] != z) | (ylo != y) | (i != chip))
            def _():
                remote(hub.at[0], got.at[e, y, i], a_ssem.at[0, 0], a_rsem.at[e, y, i], row, mate).wait_recv()

            return 0

        lax.fori_loop(0, 8, a_recv, 0)

    for e in range(2):
        for y in range(2):
            arrive(e, y)

    for e in range(2):
        for y in range(2):
            at = (2 * e + y) * ROWS
            rows = got[e, y, :, 0:64, :].reshape(ROWS, 128)
            turned[:, at : at + ROWS] = lax.dot_general(eye, rows, NT, preferred_element_type=F32)
            for g in range(4):
                low_f32[:, at + g * 128 : at + g * 128 + 128] = (
                    got[e, y, 2 * g, 64:80, :].astype(F32) + got[e, y, 2 * g + 1, 64:80, :].astype(F32)
                )

    left_e[...] = (turned[0:64, :] * turned[64:128, :]).astype(BF)

    def place(n, i, size):
        quarter = lax.rem(lax.div(z, 4) + QUARTERS[n][0] + 2 * lax.div(i, size), 4)
        return quarter * size + lax.rem(i, size)

    def build(n):
        bands_here = 3 * len(QUARTERS[n])

        def step(m, _):
            tile = turned[pl.ds(pl.multiple_of(m * 8, 8), 8), :]
            for p in range(SENT[n] // 16):
                pair = [
                    tile * low_f32[pl.ds(place(n, i, 3), 1), :] if i < bands_here else jnp.zeros_like(tile)
                    for i in (2 * p, 2 * p + 1)
                ]
                rows = pl.ds(pl.multiple_of(m * SENT[n] + 16 * p, 16), 16)
                left[rows, :] = jnp.concatenate(pair, axis=0).astype(BF)
            return 0

        lax.fori_loop(0, 8, step, 0)

    buffers = ((send0, recv0), (send1, recv1), (send2, recv2))

    def b_copy_to(n, m):
        sends, recvs = buffers[n]
        return remote(sends.at[m], recvs.at[chip], b_ssem.at[n, m], b_rsem.at[n, chip], row, 8 * core + m)

    for n in range(3):
        sends, recvs = buffers[n]
        build(n)

        def mul(t, _, n=n, sends=sends):
            span = pl.ds(pl.multiple_of(t * 256, 256), 256)
            size = SENT[n]
            d = jnp.dot(left[0 : 8 * size, :], w_turned[:, span], preferred_element_type=F32)
            if n == 0:
                e = jnp.dot(left_e[...], b_turned[:, span], preferred_element_type=F32)
                for m in range(8):
                    both = jnp.concatenate([d[m * size : m * size + 24], e[m * 8 : m * 8 + 8]], axis=0)
                    sends[m, :, span] = both.astype(BF)
            else:
                d = d.astype(BF)
                for m in range(8):
                    sends[m, :, span] = d[m * size : (m + 1) * size, :]
            return 0

        lax.fori_loop(0, 2, mul, 0)

        def b_start(m, _, n=n, sends=sends, recvs=recvs):
            @pl.when(8 * core + m != col)
            def _():
                b_copy_to(n, m).start()

            @pl.when(8 * core + m == col)
            def _():
                recvs[pl.ds(chip, 1)] = sends[pl.ds(m, 1)]

            return 0

        lax.fori_loop(0, 8, b_start, 0)

    points = g_all[...].reshape(ROWS, NBP)

    def b_recv(n):
        recvs = buffers[n][1]

        def step(k, _):
            @pl.when(2 * k + lax.div(col, 8) != col)
            def _():
                remote(recvs.at[k], recvs.at[k], b_ssem.at[n, 0], b_rsem.at[n, k], row, mate).wait_recv()

            return 0

        lax.fori_loop(0, 8, step, 0)

    def c_copy(i):
        return remote(seg_out.at[i], seg_in.at[z], c_ssem.at[i], c_rsem.at[z], 2 * i + ylo, col)

    lane = iota((8, SEGP), 1)
    for n in range(3):
        recvs = buffers[n][1]
        count = 3 * len(QUARTERS[n])
        b_recv(n)
        d = recvs[0].astype(F32)
        for k in range(1, 8):
            d = d + recvs[k].astype(F32)
        if n == 0:
            exch = 2.0 * d[24:32]
        comb = [
            row_low[pl.ds(place(n, i, 3), 1), :] * exch - row_vp[...] * d[i * 8 : i * 8 + 8] for i in range(count)
        ]
        if count == 3:
            comb.append(jnp.zeros_like(exch))
        comb = jnp.concatenate(comb, axis=0)
        head = comb.astype(BF)
        rest = (comb - head.astype(F32)).astype(BF)
        panel[0 : SENT[n], :] = jnp.dot(head, points, preferred_element_type=F32) + jnp.dot(
            rest, points, preferred_element_type=F32
        )
        for zl in range(4 * len(QUARTERS[n])):
            halves = []
            for y in range(2):
                start = SEG * (2 * zl + y)
                band0, off = start // NB, start % NB
                seg = panel[band0 * 8 : band0 * 8 + 8, :]
                if off:
                    seg = pltpu.roll(seg, NBP - off, 1)
                seg = seg[:, 0:SEGP]
                if off + SEG > NB:
                    more = pltpu.roll(panel[band0 * 8 + 8 : band0 * 8 + 16, :], NB - off, 1)[:, 0:SEGP]
                    seg = jnp.where(lane < NB - off, seg, more)
                halves.append(seg)
            seg_out[pl.ds(place(n, jnp.int32(zl), 4), 1)] = jnp.concatenate(halves, axis=0).astype(BF).reshape(1, 16, SEGP)

        def c_start(i, _, n=n):
            there = place(n, i, 4)

            @pl.when(there != z)
            def _():
                c_copy(there).start()

            @pl.when(there == z)
            def _():
                seg_in[pl.ds(z, 1)] = seg_out[pl.ds(z, 1)]

            return 0

        lax.fori_loop(0, 4 * len(QUARTERS[n]), c_start, 0)

    def c_recv(i, _):
        @pl.when(i != z)
        def _():
            remote(seg_out.at[i], seg_in.at[i], c_ssem.at[i], c_rsem.at[i], row, mate).wait_recv()

        return 0

    lax.fori_loop(0, NZ, c_recv, 0)
    acc = seg_in[0].astype(F32)
    for i in range(1, NZ):
        acc = acc + seg_in[i].astype(F32)
    total[...] = acc.reshape(2, 8, SEGP)
    y_copy = remote(total.at[1 - ylo], y_in, y_ssem, y_rsem, other_row, col)
    y_copy.start()

    def drain(i, _):
        @pl.when(i != z)
        def _():
            c_copy(i).wait_send()

        return 0

    lax.fori_loop(0, NZ, drain, 0)
    for n in range(1, 5):
        s_copy(n).wait_send()
    for m in range(len(SECOND)):
        for y in range(2):
            own = a_to_self(m, y)
            if own is None:
                a_copy(m, y).wait_send()
            else:
                @pl.when(jnp.logical_not(own))
                def _(m=m, y=y):
                    a_copy(m, y).wait_send()

    def drain8(i, _):
        @pl.when(i != chip)
        def _():
            g_copy(i).wait_send()

        h_copy(i, core).wait_send()

        @pl.when(8 * core + i != col)
        def _():
            for n in range(3):
                b_copy_to(n, i).wait_send()

        return 0

    lax.fori_loop(0, 8, drain8, 0)
    swap.wait_send()
    w_copy.wait_send()
    b_copy.wait_send()
    y_copy.wait()
    out_ref[...] = total[ylo] + y_in[...]


def body(orb_valence, orb_conduction, screened, bare, panel_valence, panel_conduction):
    vmem = pl.BlockSpec(memory_space=pltpu.VMEM)
    hbm = pl.BlockSpec(memory_space=pl.ANY)
    dma = pltpu.SemaphoreType.DMA
    out = pl.pallas_call(
        kernel,
        out_shape=jax.ShapeDtypeStruct((8, SEGP), F32),
        in_specs=[hbm] * 6,
        out_specs=vmem,
        scratch_shapes=[
            pltpu.VMEM((PTS, NB), BF),
            pltpu.VMEM((PTS, NB), BF),
            pltpu.VMEM((1, 128), jnp.int32),
            pltpu.VMEM((1, 128), jnp.int32),
            pltpu.VMEM((5, 80, 128), BF),
            pltpu.VMEM((128, NB), BF),
            pltpu.VMEM((NCOL, PTS, NBP), BF),
            pltpu.VMEM((16, ROWS), F32),
            pltpu.VMEM((8, ROWS), F32),
            pltpu.VMEM((48, 128), BF),
            pltpu.VMEM((48, 128), BF),
            pltpu.VMEM((2, 2, 8, 80, 128), BF),
            pltpu.VMEM((16, 2 * COLS), F32),
            pltpu.VMEM((128, 2 * COLS), F32),
            pltpu.VMEM((8 * 48, 2 * COLS), BF),
            pltpu.VMEM((64, 2 * COLS), BF),
            pltpu.VMEM((2, ROWS, COLS), BF),
            pltpu.VMEM((2, ROWS, COLS), BF),
            pltpu.VMEM((2 * COLS, ROWS), BF),
            pltpu.VMEM((2 * COLS, ROWS), BF),
            pltpu.VMEM((8, 32, ROWS), BF),
            pltpu.VMEM((8, 48, ROWS), BF),
            pltpu.VMEM((8, 32, ROWS), BF),
            pltpu.VMEM((8, 32, ROWS), BF),
            pltpu.VMEM((8, 48, ROWS), BF),
            pltpu.VMEM((8, 32, ROWS), BF),
            pltpu.VMEM((48, NBP), F32),
            pltpu.VMEM((NZ, 16, SEGP), BF),
            pltpu.VMEM((NZ, 16, SEGP), BF),
            pltpu.VMEM((2, 8, SEGP), F32),
            pltpu.VMEM((8, SEGP), F32),
            dma((6,)),
            dma((2,)), dma((2,)),
            dma((len(SECOND), 2)), dma((2, 2, 8)),
            dma((5,)), dma((5,)),
            dma((8,)), dma((8,)),
            dma((8,)), dma((8,)),
            dma, dma,
            dma((3, 8)), dma((3, 8)),
            dma((16,)), dma((16,)),
            dma, dma,
        ],
        compiler_params=pltpu.CompilerParams(
            collective_id=0, has_side_effects=True, vmem_limit_bytes=60 * 2**20
        ),
        name="kernel_panel",
    )(
        orb_valence, orb_conduction, panel_valence.reshape(1, -1), panel_conduction.reshape(1, -1),
        screened, bare,
    )
    return out[:, :SEG].T


def solution(mesh):
    placed = (
        P(("prow", "pcol"), None),
        P(("prow", "pcol"), None),
        P("prow", "pcol"),
        P("prow", "pcol"),
        P(),
        P(),
    )
    return jax.shard_map(
        body, mesh=mesh, in_specs=placed, out_specs=P("prow", "pcol"), check_vma=False
    )
```
